32 devices in a mesh: context: 2 (over y), tensor: 4 (over z), fsdp: 4 (over x, core).
Axes of the slice: x: 2, y: 2, z: 4, core: 2. Of those that a mesh axis runs over, the one named last changes fastest.
Arguments:
- queries: bfloat16 [4, 256, 4096], P('fsdp', 'context', 'tensor'), may hold values from -8 to 8
- keys: bfloat16 [4, 256, 4096], P('fsdp', 'context', 'tensor'), may hold values from -8 to 8
- values: bfloat16 [4, 256, 4096], P('fsdp', 'context', 'tensor'), may hold values from -6 to 6
- out_grad: bfloat16 [4, 256, 4096], P('fsdp', 'context', 'tensor'), may hold values from -6 to 6
- out_weight: bfloat16 [4096, 4096], P('fsdp', 'tensor'), may hold values from -0.09375 to 0.09375
- slopes: float32 [32], P('tensor'), may hold values from 0.00048828125 to 0.05
- counts: int32 [4, 2], P('fsdp', 'context'), may hold values from 1 to 128, 160 in all within a row
- gaps: int32 [4, 256], P('fsdp', 'context'), may hold values from 1 to 12
Outputs:
- query_grad: bfloat16 [4, 256, 4096], P('fsdp', 'context', 'tensor')
- key_grad: bfloat16 [4, 256, 4096], P('fsdp', 'context', 'tensor')
- value_grad: bfloat16 [4, 256, 4096], P('fsdp', 'context', 'tensor')
- weight_grad: float32 [4096, 4096], P('fsdp', 'tensor')
The draws below stay inside these ranges and needn't reach their ends.
Inputs may be any that keep to these rules, and one draw needn't show every extreme that they name: In each sequence the counts sum to 160 and the largest is 128.
All inputs are finite; a program needn't handle non-finite values. No bound on the sum of `counts` on one device may be relied on, other than what follows from the above.
Results may differ from the reference program's by a relative error of at most 0.022.
Values may be sent and summed in bfloat16 or wider, within the bound.
No kernel may reach another device: no remote copies, remote signals or barrier semaphores. Data moves between devices by JAX's collectives and lax.ppermute only.
A program may use at most 64 MiB of HBM per device.

```python
import math
import jax
import jax.numpy as jnp
import numpy as np
from jax import lax

D = 4096
HEADS = 32
HEAD_DIM = 128
ROWS = 128
POSITIONS = 256
SEQS = 4
BOUNDARIES = 160
N_CONTEXT = 2


def fresh_rows(key, salt):
    return jax.random.truncated_normal(jax.random.fold_in(key, salt), -4.0, 4.0, (SEQS, POSITIONS, HEADS * HEAD_DIM), jnp.float32)


def draw_queries(key, part):
    fresh = fresh_rows(key, 1)
    return fresh.astype(jnp.bfloat16)


def draw_keys(key, part):
    fresh = fresh_rows(key, 2)
    return fresh.astype(jnp.bfloat16)


def place_ends(array, stream_key, low, high):
    longest = array.shape.index(max(array.shape))
    spots = []
    for shift in (0, 1):
        where = [jax.random.randint(jax.random.fold_in(stream_key, axis), (), 0, length) for axis, length in enumerate(array.shape)]
        where[longest] = (where[longest] + shift) % array.shape[longest]
        spots.append(tuple(where))
    return array.at[spots[0]].set(low).at[spots[1]].set(high)


def level_of(rng, shape, shards, smallest, largest):
    level, own = 1.0, jax.random.fold_in(rng, 6)
    for axis_at, shards_of in shards:
        heights = jnp.exp(jax.random.uniform(jax.random.fold_in(own, axis_at), (shards_of,), jnp.float32, smallest / len(shards), largest / len(shards)))
        level = level * jnp.repeat(heights, shape[axis_at] // shards_of).reshape([-1 if axis == axis_at else 1 for axis in range(len(shape))])
    return level


def split_up(amount, total, limit, skew):
    weights = [(1 << 20) // math.isqrt(standing ** skew) + 1 for standing in range(2, amount + 1)]
    surplus, given = total - limit - (amount - 1), [1] * (amount - 1)
    while surplus > 0:
        free = [i for i in range(amount - 1) if given[i] < limit]
        pool, budget = sum([weights[i] for i in free]), surplus
        for i in free:
            addition = min(limit - given[i], max(1, budget * weights[i] // pool), surplus)
            given[i] = given[i] + addition
            surplus = surplus - addition
    return np.array([limit] + given)


def ragged_sizes(own_key, amount, total, reach, skew):
    if amount == 2:
        one = jax.random.randint(own_key, (), max(1, total - reach), min(reach, total - 1) + 1)
        return jnp.stack([one, total - one])
    sizes = jnp.asarray(split_up(amount, total, reach, skew), jnp.int32)
    twos = (amount - 1) // 2
    giver, taker = sizes[1:1 + 2 * twos:2], sizes[2:2 + 2 * twos:2]
    room = jnp.minimum(giver - 1, reach - taker)
    moved = jax.random.randint(jax.random.fold_in(own_key, 1), (twos,), 0, 1 << 20) % (room + 1)
    sizes = sizes.at[1:1 + 2 * twos:2].set(giver - moved).at[2:2 + 2 * twos:2].set(taker + moved)
    return sizes[jax.random.permutation(jax.random.fold_in(own_key, 2), amount)]


def noise(own_key, shape, spread, reach, pieces=(), kind=jnp.bfloat16):
    level = level_of(own_key, shape, pieces, -0.22, 0.18) if pieces else 1.0
    entries = jax.random.normal(own_key, shape, jnp.float32) * spread * level
    return jnp.minimum(jnp.maximum(entries, -reach), reach).astype(kind)


def setup_inputs(seed: int = 0) -> dict:
    arg_keys = jax.random.split(jax.random.key(seed), 9)
    queries = draw_queries(jax.random.fold_in(arg_keys[8], 71), 0)
    keys = draw_keys(jax.random.fold_in(arg_keys[8], 71), 0)
    values = noise(arg_keys[2], (SEQS, POSITIONS, HEADS * HEAD_DIM), 1.0, 6.0, ((0, 4), (1, 2), (2, 4)))
    out_grad = noise(arg_keys[3], (SEQS, POSITIONS, D), 1.0, 6.0, ((0, 4), (1, 2), (2, 4)))
    out_weight = noise(arg_keys[4], (D, HEADS * HEAD_DIM), (HEADS * HEAD_DIM) ** -0.5, 0.09375, ((0, 4), (1, 4)))
    slopes = jnp.clip(jnp.exp(math.log(0.05) - 4.6288867 * jax.random.uniform(arg_keys[5], (HEADS,), jnp.float32) ** level_of(arg_keys[5], (HEADS,), ((0, 4),), -0.2, 0.2)), 0.00048828125, 0.05)
    counts = jax.vmap(lambda own: ragged_sizes(own, N_CONTEXT, BOUNDARIES, ROWS, 2))(jax.random.split(arg_keys[6], SEQS)).reshape((SEQS, N_CONTEXT)).astype(jnp.int32)
    gaps = place_ends(jax.random.randint(arg_keys[7], (SEQS, POSITIONS), 1, 13), jax.random.fold_in(arg_keys[7], 1), 1, 12).astype(jnp.int32)
    return {"queries": queries, "keys": keys, "values": values, "out_grad": out_grad, "out_weight": out_weight, "slopes": slopes, "counts": counts, "gaps": gaps}


NEG = -1e30


def split_heads(block):
    return block.reshape(POSITIONS, HEADS, HEAD_DIM).transpose(1, 0, 2)


def merge_heads(block):
    return block.transpose(1, 0, 2).reshape(POSITIONS, HEADS * HEAD_DIM)


def reference(queries, keys, values, out_grad, out_weight, slopes, counts, gaps):
    slot_index = jnp.arange(POSITIONS, dtype=jnp.int32)
    scaling = HEAD_DIM ** -0.5

    def one_sequence(inputs):
        q_seq, k_seq, v_seq, grad_seq, count_seq, gap_seq = inputs
        limits = jnp.repeat(count_seq, ROWS)
        slot_valid = (slot_index % ROWS) < limits
        offsets = jnp.cumsum(jnp.where(slot_valid, gap_seq, 0)).astype(jnp.float32)
        grad_masked = jnp.where(slot_valid[:, None], grad_seq, jnp.zeros_like(grad_seq))
        grad_heads = jnp.dot(grad_masked, out_weight, preferred_element_type=jnp.float32).astype(jnp.bfloat16)
        allowed = slot_valid[None, :] & (slot_index[None, :] <= slot_index[:, None])

        def one_head(head_inputs):
            q_head, k_head, v_head, g_head, slope = head_inputs
            logits = jnp.dot(q_head, k_head.T, preferred_element_type=jnp.float32) * scaling
            logits = logits - slope * (offsets[:, None] - offsets[None, :])
            logits = jnp.where(allowed, logits, NEG)
            peak = jnp.max(logits, axis=1)
            log_total = peak + jnp.log(jnp.sum(jnp.where(allowed, jnp.exp(logits - peak[:, None]), 0.0), axis=1))
            probs = jnp.where(allowed, jnp.exp(logits - log_total[:, None]), 0.0)
            probs_b = probs.astype(jnp.bfloat16)
            output = jnp.dot(probs_b, v_head, preferred_element_type=jnp.float32).astype(jnp.bfloat16)
            delta = jnp.sum(g_head.astype(jnp.float32) * output.astype(jnp.float32), axis=1)
            value_dots = jnp.dot(g_head, v_head.T, preferred_element_type=jnp.float32)
            dscore = (probs * (value_dots - delta[:, None])).astype(jnp.bfloat16)
            q_grad = (jnp.dot(dscore, k_head, preferred_element_type=jnp.float32) * scaling).astype(jnp.bfloat16)
            k_grad = (jnp.dot(dscore.T, q_head, preferred_element_type=jnp.float32) * scaling).astype(jnp.bfloat16)
            v_grad = jnp.dot(probs_b.T, g_head, preferred_element_type=jnp.float32).astype(jnp.bfloat16)
            return output, q_grad, k_grad, v_grad

        output, q_grad, k_grad, v_grad = lax.map(one_head, (split_heads(q_seq), split_heads(k_seq), split_heads(v_seq), split_heads(grad_heads), slopes))
        weight_term = lax.dot_general(grad_masked, merge_heads(output), (((0,), (0,)), ((), ())), preferred_element_type=jnp.float32)
        return merge_heads(q_grad), merge_heads(k_grad), merge_heads(v_grad), weight_term

    def accumulate(total, inputs):
        q_grad, k_grad, v_grad, weight_term = one_sequence(inputs)
        return total + weight_term, (q_grad, k_grad, v_grad)

    start_total = jnp.zeros((D, HEADS * HEAD_DIM), jnp.float32)
    weight_grad, grads = lax.scan(accumulate, start_total, (queries, keys, values, out_grad, counts, gaps))
    return grads[0], grads[1], grads[2], weight_grad
```

```python
import functools

import jax
import jax.numpy as jnp
from jax import lax
from jax.experimental import pallas as pl
from jax.experimental.pallas import tpu as pltpu
from jax.sharding import PartitionSpec as P

NEG = -1e30
F32 = jnp.float32
BF16 = jnp.bfloat16
NN = (((1,), (0,)), ((), ()))
NT = (((1,), (1,)), ((), ()))
TN = (((0,), (0,)), ((), ()))


def dot(a, b, dims=NN):
    return lax.dot_general(a, b, dims, preferred_element_type=F32)


def iota(shape, axis):
    return lax.broadcasted_iota(jnp.int32, shape, axis)


def onehot(mask):
    return jnp.where(mask, 1.0, 0.0).astype(BF16)


def call(body, outs, args, smem=(), scratch=(), vmem=32):
    return pl.pallas_call(
        body,
        out_shape=outs,
        in_specs=[
            pl.BlockSpec(memory_space=pltpu.SMEM if i in smem else pltpu.VMEM)
            for i in range(len(args))
        ],
        out_specs=jax.tree.map(lambda _: pl.BlockSpec(memory_space=pltpu.VMEM), outs),
        scratch_shapes=list(scratch),
        compiler_params=pltpu.CompilerParams(vmem_limit_bytes=vmem * 2**20),
    )(*args)


def packed_slot(index, half, rows, count0, count1):
    own0 = jnp.where(index < count0, index, rows + half + index - count0)
    other = index - half
    own1 = jnp.where(other < count1, rows + other, half + other - count1)
    return jnp.where(index < half, own0, own1)


def pack_message_kernel(q_ref, k_ref, v_ref, gaps_ref, out_ref):
    rows, width = q_ref.shape
    part = width // 2
    away = pl.ds(pl.multiple_of((1 - lax.axis_index("context")) * part, part), part)
    for n, ref in enumerate((q_ref, k_ref, v_ref)):
        out_ref[n * rows : (n + 1) * rows, :] = ref[:, away]
    tail = jnp.zeros((16, part), F32)
    line = jnp.broadcast_to(gaps_ref[...].astype(F32), (16, rows))
    out_ref[3 * rows :, :] = tail.astype(BF16)
    out_ref[3 * rows :, :rows] = line.astype(BF16)


def pack_rows_kernel(count_ref, own_ref, extra_ref, out_ref):
    half = out_ref.shape[0]
    extra = extra_ref.shape[0]
    count = count_ref[0, 0]
    at, row = iota((half, half), 0), iota((half, half), 1)
    first = onehot((at == row) & (at < count))
    at, row = iota((half, extra), 0), iota((half, extra), 1)
    second = onehot((at >= count) & (at - count == row))
    out_ref[...] = (dot(first, own_ref[:half, :]) + dot(second, extra_ref[...])).astype(BF16)


def forward_kernel(
    count_ref, slopes_ref, q_ref, k_ref, v_ref, gaps_ref, message_ref,
    q_out, k_out, v_out, probs_out, output_ref,
):
    rows, width = q_ref.shape
    part = width // 2
    total = q_out.shape[0]
    half = total // 2
    heads = probs_out.shape[0]
    size = part // heads
    c = lax.axis_index("context")
    count = count_ref[0, 0]
    count0 = jnp.where(c == 0, count, total - count)
    count1 = total - count0
    slot_down = packed_slot(iota((total, rows), 0), half, rows, count0, count1)
    slot_here = iota((total, rows), 1)
    own_slot = c * rows + slot_here
    peer_slot = (1 - c) * rows + slot_here
    own_pick, peer_pick = onehot(slot_down == own_slot), onehot(slot_down == peer_slot)
    own_until = onehot((own_slot <= slot_down) & (slot_here < count))
    peer_until = onehot((peer_slot <= slot_down) & (slot_here < total - count))
    own_gaps = jnp.broadcast_to(gaps_ref[...].astype(F32), (16, rows)).astype(BF16)
    peer_gaps = message_ref[3 * rows :, :rows]
    offset_down = (dot(own_until, own_gaps, NT) + dot(peer_until, peer_gaps, NT))[:, :1]
    offset_across = (dot(own_gaps, own_until, NT) + dot(peer_gaps, peer_until, NT))[:1, :]
    slot_q = packed_slot(iota((total, total), 0), half, rows, count0, count1)
    slot_k = packed_slot(iota((total, total), 1), half, rows, count0, count1)
    allowed = slot_k <= slot_q
    distance = offset_down - offset_across
    mine = pl.ds(pl.multiple_of(c * part, part), part)
    for n, (ref, out) in enumerate(((q_ref, q_out), (k_ref, k_out), (v_ref, v_out))):
        out[...] = (
            dot(own_pick, ref[:, mine]) + dot(peer_pick, message_ref[n * rows : (n + 1) * rows, :])
        ).astype(BF16)
    for h in range(heads):
        cols = slice(h * size, (h + 1) * size)
        slope = slopes_ref[0, c * heads + h]
        score = dot(q_out[:, cols], k_out[:, cols], NT) * (size**-0.5) - slope * distance
        score = jnp.where(allowed, score, NEG)
        peak = jnp.max(score, axis=1, keepdims=True)
        mass = jnp.where(allowed, jnp.exp(score - peak), 0.0)
        probs = mass / jnp.sum(mass, axis=1, keepdims=True)
        probs_out[h] = probs
        output_ref[:, cols] = dot(probs.astype(BF16), v_out[:, cols]).astype(BF16)


def partial_kernel(
    b00_ref, b01_ref, b10_ref, b11_ref, own_w_ref, near_w_ref,
    partial_ref, send_ref, own_g_ref, near_g_ref,
):
    half = send_ref.shape[0]
    t, f = lax.axis_index("tensor"), lax.axis_index("fsdp")
    h, l, x, core = t // 2, t % 2, f // 2, f % 2
    swap_seq = (h + x) % 2 == 1
    swap_chunk = (l + core) % 2 == 1

    def pick(a, b, swap):
        return jnp.where(swap, b[...], a[...])

    def place(own00, own01, own10, own11):
        own_g_ref[:half], near_g_ref[:half] = own00[...], own01[...]
        own_g_ref[half:], near_g_ref[half:] = own10[...], own11[...]

    for seq in (False, True):
        for chunk in (False, True):
            blocks = ((b00_ref, b01_ref), (b10_ref, b11_ref))
            first, second = blocks[seq], blocks[not seq]

            @pl.when((swap_seq == seq) & (swap_chunk == chunk))
            def _(first=first, second=second, chunk=chunk):
                place(first[chunk], first[not chunk], second[chunk], second[not chunk])

    total = dot(own_g_ref[...], own_w_ref[...]) + dot(near_g_ref[...], near_w_ref[...])
    partial_ref[...] = total[:half]
    send_ref[...] = total[half:].astype(BF16)


def backward_kernel(
    count_ref, q_ref, k_ref, v_ref, probs_ref, output_ref, partial_ref, arrived_ref, peer_ref,
    own_ref, send_ref, g_ref, grads_ref,
):
    total, part = q_ref.shape
    half = total // 2
    heads = probs_ref.shape[0]
    size = part // heads
    rows = own_ref.shape[0] // 3
    c = lax.axis_index("context")
    count = count_ref[0, 0]
    count0 = jnp.where(c == 0, count, total - count)
    mine = pl.ds(pl.multiple_of(c * part, part), part)
    here = (partial_ref[:, mine] + arrived_ref[:, mine].astype(F32)).astype(BF16)
    g_ref[pl.ds(pl.multiple_of(c * half, half), half), :] = here
    g_ref[pl.ds(pl.multiple_of((1 - c) * half, half), half), :] = peer_ref[...]
    for h in range(heads):
        cols = slice(h * size, (h + 1) * size)
        probs = probs_ref[h]
        g, q, k, v = g_ref[:, cols], q_ref[:, cols], k_ref[:, cols], v_ref[:, cols]
        delta = jnp.sum(g.astype(F32) * output_ref[:, cols].astype(F32), axis=1, keepdims=True)
        dscore = (probs * (dot(g, v, NT) - delta)).astype(BF16)
        grads_ref[0, :, cols] = (dot(dscore, k) * (size**-0.5)).astype(BF16)
        grads_ref[1, :, cols] = (dot(dscore, q, TN) * (size**-0.5)).astype(BF16)
        grads_ref[2, :, cols] = dot(probs.astype(BF16), g, TN).astype(BF16)
    slot = packed_slot(iota((rows, total), 1), half, rows, count0, total - count0)
    row = iota((rows, total), 0)
    own_pick, peer_pick = onehot(slot == c * rows + row), onehot(slot == (1 - c) * rows + row)
    for n in range(3):
        send_ref[n * rows : (n + 1) * rows, :] = dot(peer_pick, grads_ref[n]).astype(BF16)
        own_ref[n * rows : (n + 1) * rows, :] = dot(own_pick, grads_ref[n]).astype(BF16)


def finish_kernel(own_ref, peer_ref, q_ref, k_ref, v_ref):
    rows, width = q_ref.shape
    part = width // 2
    c = lax.axis_index("context")
    mine = pl.ds(pl.multiple_of(c * part, part), part)
    away = pl.ds(pl.multiple_of((1 - c) * part, part), part)
    for n, ref in enumerate((q_ref, k_ref, v_ref)):
        ref[:, mine] = own_ref[n * rows : (n + 1) * rows, :]
        ref[:, away] = peer_ref[n * rows : (n + 1) * rows, :]


def weight_kernel(
    own_g_ref, near_g_ref, peer_g_ref, out_a_ref, out_b_ref, out_ref, right_ref, left_ref
):
    pair = own_g_ref.shape[0]
    half = pair // 2
    part = right_ref.shape[1] // 2
    total = 2 * half

    @pl.when(pl.program_id(0) == 0)
    def _():
        c = lax.axis_index("context")
        for s in range(4):
            source = out_a_ref if s < 2 else out_b_ref
            for side in range(2):
                base = ((s % 2) * 2 + side) * total
                at = pl.ds(pl.multiple_of((c if side == 0 else 1 - c) * part, part), part)
                for which in range(2):
                    rows = (c if which == 0 else 1 - c) * half + base
                    to = (which * 4 + s) * half
                    right_ref[to : to + half, at] = source[
                        pl.ds(pl.multiple_of(rows, half), half), :
                    ]

    left_ref[:pair, :] = own_g_ref[...]
    left_ref[pair : 2 * pair, :] = near_g_ref[...]
    left_ref[2 * pair :, :] = peer_g_ref[...]
    out_ref[...] = dot(left_ref[...], right_ref[...], TN)


def weight_gradient(own_g, near_g, peer_g, out_a, out_b, blocks=4):
    pair, features = own_g.shape
    width = 2 * out_a.shape[1]
    block = features // blocks
    column = lambda i: (0, i)
    whole = lambda i: (0, 0)
    return pl.pallas_call(
        weight_kernel,
        grid=(blocks,),
        out_shape=jax.ShapeDtypeStruct((features, width), F32),
        in_specs=[
            pl.BlockSpec((pair, block), column),
            pl.BlockSpec((pair, block), column),
            pl.BlockSpec((2 * pair, block), column),
            pl.BlockSpec(out_a.shape, whole),
            pl.BlockSpec(out_b.shape, whole),
        ],
        out_specs=pl.BlockSpec((block, width), lambda i: (i, 0)),
        scratch_shapes=[pltpu.VMEM((4 * pair, width), BF16), pltpu.VMEM((4 * pair, block), BF16)],
        compiler_params=pltpu.CompilerParams(vmem_limit_bytes=32 * 2**20),
    )(own_g, near_g, peer_g, out_a, out_b)


def spread(flip_seq, flip_chunk):
    pairs = []
    for t in range(4):
        for f in range(4):
            h, l, x, core = t >> 1, t & 1, f >> 1, f & 1
            to_t = ((x ^ flip_seq) << 1) | (l ^ flip_chunk)
            pairs.append((t * 4 + f, to_t * 4 + (h << 1 | core)))
    return pairs


def packed_device(queries, keys, values, out_grad, out_weight, slopes, counts, gaps):
    rows, width = queries.shape[1:]
    part = width // 2
    total = 2 * rows * 5 // 8
    half = total // 2
    heads = slopes.shape[0] // 2
    shape = jax.ShapeDtypeStruct
    over_y = lambda a: lax.ppermute(a, "context", [(0, 1), (1, 0)])
    over_x = lambda a: lax.ppermute(a, "fsdp", [(i, i ^ 2) for i in range(4)])
    over_core = lambda a: lax.ppermute(a, "fsdp", [(i, i ^ 1) for i in range(4)])
    slopes = slopes[None]

    grad = out_grad[0]
    extra = over_y(grad[half:])
    message = call(
        pack_message_kernel,
        shape((3 * rows + 16, part), BF16),
        (queries[0], keys[0], values[0], gaps),
    )
    message = over_y(message)
    near_weight = over_core(out_weight)
    packed = call(pack_rows_kernel, shape((half, width), BF16), (counts, grad, extra), smem=(0,))
    blocks = [
        lax.ppermute(packed, ("tensor", "fsdp"), spread(a, b)) for a in (0, 1) for b in (0, 1)
    ]
    q, k, v, probs, output = call(
        forward_kernel,
        (
            shape((total, part), BF16),
            shape((total, part), BF16),
            shape((total, part), BF16),
            shape((heads, total, total), F32),
            shape((total, part), BF16),
        ),
        (counts, slopes, queries[0], keys[0], values[0], gaps, message),
        smem=(0, 1),
    )
    peer_output = over_y(output)
    partial, send, own_g, near_g = call(
        partial_kernel,
        (
            shape((half, width), F32),
            shape((half, width), BF16),
            shape((total, width), BF16),
            shape((total, width), BF16),
        ),
        (*blocks, out_weight, near_weight),
    )
    arrived = over_x(send)
    near_g = over_core(near_g)
    both = jnp.concatenate([output, peer_output], axis=0)
    out_a = jnp.concatenate([both, over_x(both)], axis=0)
    out_b = over_core(out_a)
    c = lax.axis_index("context")
    away = (1 - c) * part
    here = lax.dynamic_slice_in_dim(partial, away, part, 1) + lax.dynamic_slice_in_dim(
        arrived, away, part, 1
    ).astype(F32)
    peer_head = over_y(here.astype(BF16))
    peer_g = over_y(jnp.concatenate([own_g, near_g], axis=0))
    own, send = call(
        backward_kernel,
        (shape((3 * rows, part), BF16), shape((3 * rows, part), BF16)),
        (counts, q, k, v, probs, output, partial, arrived, peer_head),
        smem=(0,),
        scratch=(pltpu.VMEM((total, part), BF16), pltpu.VMEM((3, total, part), BF16)),
    )
    peer = over_y(send)
    weight_grad = weight_gradient(own_g, near_g, peer_g, out_a, out_b)
    grads = call(finish_kernel, tuple(shape((rows, width), BF16) for _ in range(3)), (own, peer))
    return (grads[0][None], grads[1][None], grads[2][None], weight_grad)


def general_device(queries, keys, values, out_grad, out_weight, slopes, counts, gaps):
    row_count = queries.shape[1]
    width = queries.shape[2]
    head_count = slopes.shape[0]
    head_size = width // head_count
    scaling = head_size ** (-0.5)
    shard_count = lax.axis_size("context")
    my_start = lax.axis_index("context") * row_count
    total_slots = shard_count * row_count
    all_gaps, all_counts = (
        lax.all_gather(gaps, "context", axis=1, tiled=True),
        lax.all_gather(counts, "context", axis=1, tiled=True),
    )
    slot_index = jnp.arange(total_slots, dtype=jnp.int32)
    owner = slot_index // row_count
    shard_ids = jnp.arange(shard_count, dtype=jnp.int32)
    slot_limit = jnp.sum(
        jnp.where(owner[:, None] == shard_ids[None, :], all_counts[0][None, :], 0), axis=1
    )
    slot_valid = slot_index % row_count < slot_limit
    offsets = jnp.cumsum(jnp.where(slot_valid, all_gaps[0], 0)).astype(jnp.float32)
    my_valid = lax.dynamic_slice_in_dim(slot_valid, my_start, row_count)
    grad_full = lax.all_gather(out_grad[0], "tensor", axis=1, tiled=True)
    grad_masked = jnp.where(my_valid[:, None], grad_full, jnp.zeros_like(grad_full))
    columns = grad_masked
    grad_heads = jnp.dot(
        columns,
        lax.all_gather(out_weight, "fsdp", axis=0, tiled=True),
        preferred_element_type=jnp.float32,
    ).astype(jnp.bfloat16)
    local_q = queries[0]
    local_k = keys[0]
    local_v = values[0]
    key_full, value_full = (
        lax.all_gather(local_k, "context", axis=0, tiled=True),
        lax.all_gather(local_v, "context", axis=0, tiled=True),
    )

    def split(block):
        return block.reshape(block.shape[0], head_count, head_size)

    def scores(q_block, q_start, k_block, k_start):
        query_count = q_block.shape[0]
        key_count = k_block.shape[0]
        logits = (
            jnp.einsum(
                "qhd,khd->hqk", split(q_block), split(k_block), preferred_element_type=jnp.float32
            )
            * scaling
        )
        q_offset = lax.dynamic_slice_in_dim(offsets, q_start, query_count)
        k_offset = lax.dynamic_slice_in_dim(offsets, k_start, key_count)
        k_valid = lax.dynamic_slice_in_dim(slot_valid, k_start, key_count)
        q_slot = q_start + jnp.arange(query_count, dtype=jnp.int32)
        k_slot = k_start + jnp.arange(key_count, dtype=jnp.int32)
        allowed = k_valid[None, :] & (k_slot[None, :] <= q_slot[:, None])
        logits = logits - slopes[:, None, None] * (
            q_offset[None, :, None] - k_offset[None, None, :]
        )
        return (jnp.where(allowed[None], logits, NEG), allowed)

    def tile_terms(q_block, g_block, q_lse, q_delta, q_start, k_block, v_block, k_start):
        logits, allowed = scores(q_block, q_start, k_block, k_start)
        probs = jnp.where(allowed[None], jnp.exp(logits - q_lse[:, :, None]), 0.0)
        value_dots = jnp.einsum(
            "qhd,khd->hqk", split(g_block), split(v_block), preferred_element_type=jnp.float32
        )
        dscore = (probs * (value_dots - q_delta[:, :, None])).astype(jnp.bfloat16)
        return (probs.astype(jnp.bfloat16), dscore)

    block = 2 * row_count
    block_total = total_slots // block

    def mass_step(block_index, carry):
        k_start = block_index * block
        k_block = lax.dynamic_slice_in_dim(key_full, k_start, block, 0)

        def work(state):
            peak, mass = state
            logits, allowed = scores(local_q, my_start, k_block, k_start)
            new_peak = jnp.maximum(peak, jnp.max(logits, axis=2))
            weights = jnp.where(allowed[None], jnp.exp(logits - new_peak[:, :, None]), 0.0)
            return (new_peak, mass * jnp.exp(peak - new_peak) + jnp.sum(weights, axis=2))

        return work(carry)

    start_state = (
        jnp.full((head_count, row_count), NEG, jnp.float32),
        jnp.zeros((head_count, row_count), jnp.float32),
    )
    peak, mass = lax.fori_loop(0, block_total, mass_step, start_state)
    log_total = peak + jnp.log(mass)

    def output_step(block_index, carry):
        k_start = block_index * block
        k_block = lax.dynamic_slice_in_dim(key_full, k_start, block, 0)
        v_block = lax.dynamic_slice_in_dim(value_full, k_start, block, 0)

        def work(acc):
            logits, allowed = scores(local_q, my_start, k_block, k_start)
            probs_b = jnp.where(allowed[None], jnp.exp(logits - log_total[:, :, None]), 0.0).astype(
                jnp.bfloat16
            )
            return acc + jnp.einsum(
                "hqk,khd->qhd", probs_b, split(v_block), preferred_element_type=jnp.float32
            ).reshape(row_count, width)

        return work(carry)

    output_b = lax.fori_loop(
        0, block_total, output_step, jnp.zeros((row_count, width), jnp.float32)
    ).astype(jnp.bfloat16)
    delta = jnp.sum(
        (grad_heads.astype(jnp.float32) * output_b.astype(jnp.float32)).reshape(
            row_count, head_count, head_size
        ),
        axis=2,
    ).T

    def query_step(block_index, carry):
        k_start = block_index * block
        k_block = lax.dynamic_slice_in_dim(key_full, k_start, block, 0)
        v_block = lax.dynamic_slice_in_dim(value_full, k_start, block, 0)

        def work(acc):
            probs_b, dscore = tile_terms(
                local_q, grad_heads, log_total, delta, my_start, k_block, v_block, k_start
            )
            return (
                acc
                + jnp.einsum(
                    "hqk,khd->qhd", dscore, split(k_block), preferred_element_type=jnp.float32
                ).reshape(row_count, width)
                * scaling
            )

        return work(carry)

    query_grad = lax.fori_loop(
        0, block_total, query_step, jnp.zeros((row_count, width), jnp.float32)
    ).astype(jnp.bfloat16)
    stats_lse, stats_delta = (
        lax.all_gather(log_total, "context", axis=1, tiled=True),
        lax.all_gather(delta, "context", axis=1, tiled=True),
    )
    start = jnp.int32(0)
    q_piece = lax.all_gather(local_q, "context", axis=0, tiled=True)
    g_piece = lax.all_gather(grad_heads, "context", axis=0, tiled=True)

    def work(held):
        probs_b, dscore = tile_terms(
            q_piece, g_piece, stats_lse, stats_delta, start, local_k, local_v, my_start
        )
        key_part = (
            jnp.einsum(
                "hqk,qhd->khd", dscore, split(q_piece), preferred_element_type=jnp.float32
            ).reshape(row_count, width)
            * scaling
        )
        value_part = jnp.einsum(
            "hqk,qhd->khd", probs_b, split(g_piece), preferred_element_type=jnp.float32
        ).reshape(row_count, width)
        return jnp.concatenate([key_part, value_part], axis=1)

    key_value_grads = work(jnp.zeros((row_count, 2 * width), jnp.float32))
    key_grad = key_value_grads[:, :width].astype(jnp.bfloat16)
    value_grad = key_value_grads[:, width:].astype(jnp.bfloat16)
    columns = grad_masked
    weight_share = lax.psum_scatter(
        lax.dot_general(
            columns, output_b, (((0,), (0,)), ((), ())), preferred_element_type=jnp.float32
        ),
        "fsdp",
        scatter_dimension=0,
        tiled=True,
    )
    weight_grad = lax.psum(weight_share, "context")
    return (query_grad[None], key_grad[None], value_grad[None], weight_grad)


def solution(mesh):
    placed = (
        P("fsdp", "context", "tensor"),
        P("fsdp", "context", "tensor"),
        P("fsdp", "context", "tensor"),
        P("fsdp", "context", "tensor"),
        P("fsdp", "tensor"),
        P("tensor"),
        P("fsdp", "context"),
        P("fsdp", "context"),
    )
    sizes = dict(mesh.shape)
    packs = sizes["context"] == 2 and sizes["tensor"] == 4 and sizes["fsdp"] == 4
    return jax.shard_map(
        packed_device if packs else general_device,
        mesh=mesh,
        in_specs=placed,
        out_specs=(
            P("fsdp", "context", "tensor"),
            P("fsdp", "context", "tensor"),
            P("fsdp", "context", "tensor"),
            P("fsdp", "tensor"),
        ),
        check_vma=False,
    )
```

```python
import functools

import jax
import jax.numpy as jnp
from jax import lax
from jax.experimental import pallas as pl
from jax.experimental.pallas import tpu as pltpu
from jax.sharding import PartitionSpec as P

NEG = -1e30
F32 = jnp.float32
BF16 = jnp.bfloat16
NN = (((1,), (0,)), ((), ()))
NT = (((1,), (1,)), ((), ()))
TN = (((0,), (0,)), ((), ()))


def dot(a, b, dims=NN):
    return lax.dot_general(a, b, dims, preferred_element_type=F32)


def iota(shape, axis):
    return lax.broadcasted_iota(jnp.int32, shape, axis)


def onehot(mask):
    return jnp.where(mask, 1.0, 0.0).astype(BF16)


def call(body, outs, args, smem=(), hbm=(), scratch=(), vmem=8):
    where = {i: pltpu.SMEM for i in smem} | {i: pltpu.HBM for i in hbm}
    return pl.pallas_call(
        body,
        out_shape=outs,
        in_specs=[pl.BlockSpec(memory_space=where.get(i, pltpu.VMEM)) for i in range(len(args))],
        out_specs=jax.tree.map(lambda _: pl.BlockSpec(memory_space=pltpu.VMEM), outs),
        scratch_shapes=list(scratch),
        compiler_params=pltpu.CompilerParams(vmem_limit_bytes=vmem * 2**20),
    )(*args)


def packed_slot(index, half, rows, count0, count1):
    own0 = jnp.where(index < count0, index, rows + half + index - count0)
    other = index - half
    own1 = jnp.where(other < count1, rows + other, half + other - count1)
    return jnp.where(index < half, own0, own1)


def pack_message_kernel(
    q_ref, k_ref, v_ref, grad_ref, weight_ref, gaps_ref,
    mine_ref, away_ref, grad_here, weight_here, gaps_here, sems, others,
):
    rows, width = q_ref.shape
    part = width // 2
    c = lax.axis_index("context")
    copies = [
        pltpu.make_async_copy(gaps_ref, gaps_here, others.at[0]),
        pltpu.make_async_copy(grad_ref.at[: grad_here.shape[0], :], grad_here, others.at[1]),
        pltpu.make_async_copy(weight_ref, weight_here, others.at[2]),
    ]
    for side, out in enumerate((mine_ref, away_ref)):
        at = pl.ds(pl.multiple_of((c if side == 0 else 1 - c) * part, part), part)
        for n, ref in enumerate((q_ref, k_ref, v_ref)):
            to = out.at[n * rows : (n + 1) * rows, :]
            copies.append(pltpu.make_async_copy(ref.at[:, at], to, sems.at[side, n]))
    for copy in copies:
        copy.start()
    for copy in copies:
        copy.wait()
    line = jnp.broadcast_to(gaps_here[...].astype(F32), (16, rows)).astype(BF16)
    for out in (mine_ref, away_ref):
        out[3 * rows :, :] = jnp.zeros((16, part), BF16)
        out[3 * rows :, :rows] = line


def pack_rows_kernel(count_ref, own_ref, extra_ref, out_ref):
    half = out_ref.shape[0]
    extra = extra_ref.shape[0]
    count = count_ref[0, 0]
    at, row = iota((half, half), 0), iota((half, half), 1)
    first = onehot((at == row) & (at < count))
    at, row = iota((half, extra), 0), iota((half, extra), 1)
    second = onehot((at >= count) & (at - count == row))
    out_ref[...] = (dot(first, own_ref[...]) + dot(second, extra_ref[...])).astype(BF16)


def forward_kernel(
    count_ref, slopes_ref, mine_ref, message_ref, q_out, k_out, v_out, probs_out, output_ref
):
    part = mine_ref.shape[1]
    rows = (mine_ref.shape[0] - 16) // 3
    total = q_out.shape[0]
    half = total // 2
    heads = probs_out.shape[0]
    size = part // heads
    c = lax.axis_index("context")
    count = count_ref[0, 0]
    count0 = jnp.where(c == 0, count, total - count)
    count1 = total - count0
    slot_down = packed_slot(iota((total, rows), 0), half, rows, count0, count1)
    slot_here = iota((total, rows), 1)
    own_slot = c * rows + slot_here
    peer_slot = (1 - c) * rows + slot_here
    own_pick, peer_pick = onehot(slot_down == own_slot), onehot(slot_down == peer_slot)
    own_until = onehot((own_slot <= slot_down) & (slot_here < count))
    peer_until = onehot((peer_slot <= slot_down) & (slot_here < total - count))
    own_gaps = mine_ref[3 * rows :, :rows]
    peer_gaps = message_ref[3 * rows :, :rows]
    offset_down = (dot(own_until, own_gaps, NT) + dot(peer_until, peer_gaps, NT))[:, :1]
    offset_across = (dot(own_gaps, own_until, NT) + dot(peer_gaps, peer_until, NT))[:1, :]
    slot_q = packed_slot(iota((total, total), 0), half, rows, count0, count1)
    slot_k = packed_slot(iota((total, total), 1), half, rows, count0, count1)
    allowed = slot_k <= slot_q
    distance = offset_down - offset_across
    for n, out in enumerate((q_out, k_out, v_out)):
        at = slice(n * rows, (n + 1) * rows)
        out[...] = (dot(own_pick, mine_ref[at, :]) + dot(peer_pick, message_ref[at, :])).astype(BF16)
    for h in range(heads):
        cols = slice(h * size, (h + 1) * size)
        slope = slopes_ref[c * heads + h]
        score = dot(q_out[:, cols], k_out[:, cols], NT) * (size**-0.5) - slope * distance
        score = jnp.where(allowed, score, NEG)
        peak = jnp.max(score, axis=1, keepdims=True)
        mass = jnp.where(allowed, jnp.exp(score - peak), 0.0)
        probs = mass / jnp.sum(mass, axis=1, keepdims=True)
        probs_out[h] = probs
        output_ref[:, cols] = dot(probs.astype(BF16), v_out[:, cols]).astype(BF16)


def place(blocks, own_ref, near_ref):
    half = own_ref.shape[0] // 2
    t, f = lax.axis_index("tensor"), lax.axis_index("fsdp")
    h, l, x, core = t // 2, t % 2, f // 2, f % 2
    swap_seq = (h + x) % 2
    swap_chunk = (l + core) % 2
    for seq in range(2):
        for chunk in range(2):

            @pl.when((swap_seq == seq) & (swap_chunk == chunk))
            def _(seq=seq, chunk=chunk):
                for n in range(2):
                    at = slice(n * half, (n + 1) * half)
                    own_ref[at, :] = blocks[n ^ seq][chunk][...]
                    near_ref[at, :] = blocks[n ^ seq][1 - chunk][...]


def place_kernel(b00_ref, b01_ref, b10_ref, b11_ref, own_ref, near_ref):
    place(((b00_ref, b01_ref), (b10_ref, b11_ref)), own_ref, near_ref)


def partial_kernel(
    b00_ref, b01_ref, b10_ref, b11_ref, own_w_ref, near_w_ref,
    keep_ref, send_x_ref, send_y_ref, send_xy_ref, own_g_ref, near_g_ref, total_ref,
):
    half, part = keep_ref.shape
    place(((b00_ref, b01_ref), (b10_ref, b11_ref)), own_g_ref, near_g_ref)
    total_ref[...] = dot(own_g_ref[...], own_w_ref[...]) + dot(near_g_ref[...], near_w_ref[...])
    c = lax.axis_index("context")
    mine = pl.ds(pl.multiple_of(c * part, part), part)
    away = pl.ds(pl.multiple_of((1 - c) * part, part), part)
    keep_ref[...] = total_ref[:half, mine]
    send_x_ref[...] = total_ref[half:, mine].astype(BF16)
    send_y_ref[...] = total_ref[:half, away].astype(BF16)
    send_xy_ref[...] = total_ref[half:, away].astype(BF16)


def backward_kernel(
    count_ref, q_ref, k_ref, v_ref, probs_ref, output_ref, keep_ref, from_x_ref, from_y_ref, from_xy_ref,
    own_ref, send_ref, g_ref, grads_ref,
):
    total, part = q_ref.shape
    half = total // 2
    heads = probs_ref.shape[0]
    size = part // heads
    rows = own_ref.shape[0] // 3
    c = lax.axis_index("context")
    count = count_ref[0, 0]
    count0 = jnp.where(c == 0, count, total - count)
    here = (keep_ref[...] + from_x_ref[...].astype(F32)).astype(BF16)
    there = (from_y_ref[...].astype(F32) + from_xy_ref[...].astype(F32)).astype(BF16)
    g_ref[pl.ds(pl.multiple_of(c * half, half), half), :] = here
    g_ref[pl.ds(pl.multiple_of((1 - c) * half, half), half), :] = there
    for h in range(heads):
        cols = slice(h * size, (h + 1) * size)
        probs = probs_ref[h]
        g, q, k, v = g_ref[:, cols], q_ref[:, cols], k_ref[:, cols], v_ref[:, cols]
        delta = jnp.sum(g.astype(F32) * output_ref[:, cols].astype(F32), axis=1, keepdims=True)
        dscore = (probs * (dot(g, v, NT) - delta)).astype(BF16)
        grads_ref[0, :, cols] = (dot(dscore, k) * (size**-0.5)).astype(BF16)
        grads_ref[1, :, cols] = (dot(dscore, q, TN) * (size**-0.5)).astype(BF16)
        grads_ref[2, :, cols] = dot(probs.astype(BF16), g, TN).astype(BF16)
    slot = packed_slot(iota((rows, total), 1), half, rows, count0, total - count0)
    row = iota((rows, total), 0)
    own_pick, peer_pick = onehot(slot == c * rows + row), onehot(slot == (1 - c) * rows + row)
    for n in range(3):
        send_ref[n * rows : (n + 1) * rows, :] = dot(peer_pick, grads_ref[n]).astype(BF16)
        own_ref[n * rows : (n + 1) * rows, :] = dot(own_pick, grads_ref[n]).astype(BF16)


def finish_kernel(own_ref, peer_ref, q_ref, k_ref, v_ref):
    rows, width = q_ref.shape
    part = width // 2
    c = lax.axis_index("context")
    mine = pl.ds(pl.multiple_of(c * part, part), part)
    away = pl.ds(pl.multiple_of((1 - c) * part, part), part)
    for n, ref in enumerate((q_ref, k_ref, v_ref)):
        ref[:, mine] = own_ref[n * rows : (n + 1) * rows, :]
        ref[:, away] = peer_ref[n * rows : (n + 1) * rows, :]


def weight_kernel(
    own_g_ref, near_g_ref, own_p_ref, near_p_ref, mine_ref, mine_x_ref, mine_core_ref,
    away_ref, away_x_ref, away_core_ref, out_ref, right_ref, left_ref,
):
    pair = own_g_ref.shape[0]
    half = pair // 2
    part = right_ref.shape[1] // 2

    @pl.when(pl.program_id(0) == 0)
    def _():
        c = lax.axis_index("context")
        sides = (mine_ref, mine_x_ref, mine_core_ref), (away_ref, away_x_ref, away_core_ref)
        for side, refs in enumerate(sides):
            at = pl.ds(pl.multiple_of((c if side == 0 else 1 - c) * part, part), part)
            for s in range(4):
                source, base = refs[min(s, 2)], 2 * half * max(s - 2, 0)
                for which in range(2):
                    rows = (c if which == 0 else 1 - c) * half + base
                    to = (which * 4 + s) * half
                    right_ref[to : to + half, at] = source[
                        pl.ds(pl.multiple_of(rows, half), half), :
                    ]

    for n, ref in enumerate((own_g_ref, near_g_ref, own_p_ref, near_p_ref)):
        left_ref[n * pair : (n + 1) * pair, :] = ref[...]
    out_ref[...] = dot(left_ref[...], right_ref[...], TN)


def weight_gradient(grads, outputs, blocks=4):
    pair, features = grads[0].shape
    width = 2 * outputs[0].shape[1]
    block = features // blocks
    return pl.pallas_call(
        weight_kernel,
        grid=(blocks,),
        out_shape=jax.ShapeDtypeStruct((features, width), F32),
        in_specs=[pl.BlockSpec((pair, block), lambda i: (0, i)) for _ in grads]
        + [pl.BlockSpec(a.shape, lambda i: (0, 0)) for a in outputs],
        out_specs=pl.BlockSpec((block, width), lambda i: (i, 0)),
        scratch_shapes=[pltpu.VMEM((4 * pair, width), BF16), pltpu.VMEM((4 * pair, block), BF16)],
        compiler_params=pltpu.CompilerParams(vmem_limit_bytes=16 * 2**20),
    )(*grads, *outputs)


def spread(flip):
    pairs = []
    for t in range(4):
        for f in range(4):
            h, l, x, core = t >> 1, t & 1, f >> 1, f & 1
            pairs.append((t * 4 + f, ((x ^ flip) << 1 | l) * 4 + (h << 1 | core)))
    return pairs


def packed_device(queries, keys, values, out_grad, out_weight, slopes, counts, gaps):
    rows, width = queries.shape[1:]
    part = width // 2
    total = 2 * rows * 5 // 8
    half = total // 2
    heads = slopes.shape[0] // 2
    shape = jax.ShapeDtypeStruct
    over_y = lambda a: lax.ppermute(a, "context", [(0, 1), (1, 0)])
    over_x = lambda a: lax.ppermute(a, "fsdp", [(i, i ^ 2) for i in range(4)])
    over_core = lambda a: lax.ppermute(a, "fsdp", [(i, i ^ 1) for i in range(4)])
    after = lax.optimization_barrier

    grad = out_grad[0]
    extra = grad[half:]
    extra, q0, near_weight = after((extra, queries, out_weight))
    near_weight = over_core(near_weight)
    extra = over_y(extra)
    own_weight, grad_here = out_weight, grad[:half]
    c = lax.axis_index("context")
    tail = jnp.broadcast_to(gaps.astype(BF16), (16, rows))
    tail = jnp.concatenate([tail] * (part // rows), axis=1)

    def side(which):
        cut = lambda a: lax.dynamic_slice_in_dim(a, which * part, part, 1)
        return jnp.concatenate([cut(q0[0]), cut(keys[0]), cut(values[0]), tail], axis=0)

    mine, message = side(c), side(1 - c)
    packed = call(
        pack_rows_kernel, shape((half, width), BF16), (counts, grad_here, extra), smem=(0,)
    )
    packed, near_weight, message = after((packed, near_weight, message))
    message = over_y(message)
    first, second = [lax.ppermute(packed, ("tensor", "fsdp"), spread(a)) for a in (0, 1)]
    over_z = lambda a: lax.ppermute(a, "tensor", [(i, i ^ 1) for i in range(4)])
    blocks = [first, over_z(first), second, over_z(second)]
    q, k, v, probs, output = call(
        forward_kernel,
        (
            shape((total, part), BF16),
            shape((total, part), BF16),
            shape((total, part), BF16),
            shape((heads, total, total), F32),
            shape((total, part), BF16),
        ),
        (counts, slopes, mine, message),
        smem=(0, 1),
    )
    peer_output = over_y(output)
    peer_first, peer_second = over_y(blocks[0]), over_y(blocks[2])
    *blocks, output = after((*blocks, output))
    keep, send_x, send_y, send_xy, own_g, near_g = call(
        partial_kernel,
        (
            shape((half, part), F32),
            shape((half, part), BF16),
            shape((half, part), BF16),
            shape((half, part), BF16),
            shape((total, width), BF16),
            shape((total, width), BF16),
        ),
        (*blocks, own_weight, near_weight),
        scratch=(pltpu.VMEM((total, width), F32),),
    )
    from_xy = lax.ppermute(
        send_xy,
        ("context", "fsdp"),
        [(c * 4 + f, (1 - c) * 4 + (f ^ 2)) for c in range(2) for f in range(4)],
    )
    from_x, from_y = over_x(send_x), over_y(send_y)
    near_g = over_core(near_g)
    mine_x = over_x(output)
    mine_core = over_core(jnp.concatenate([output, mine_x], axis=0))
    from_x, from_y, from_xy, peer_output = after((from_x, from_y, from_xy, peer_output))
    away_x = over_x(peer_output)
    peer_blocks = [peer_first, over_z(peer_first), peer_second, over_z(peer_second)]
    own, send = call(
        backward_kernel,
        (shape((3 * rows, part), BF16), shape((3 * rows, part), BF16)),
        (counts, q, k, v, probs, output, keep, from_x, from_y, from_xy),
        smem=(0,),
        scratch=(pltpu.VMEM((total, part), BF16), pltpu.VMEM((3, total, part), BF16)),
    )
    peer = over_y(send)
    peer_blocks = after((send, *peer_blocks))[1:]
    own_p, near_p = call(
        place_kernel, (shape((total, width), BF16), shape((total, width), BF16)), peer_blocks
    )
    near_p = over_core(near_p)
    own_g, away_x = after((send, own_g, away_x))[1:]
    away_core = over_core(jnp.concatenate([peer_output, away_x], axis=0))
    weight_grad = weight_gradient(
        (own_g, near_g, own_p, near_p),
        (output, mine_x, mine_core, peer_output, away_x, away_core),
    )
    weight_grad, own = after((weight_grad, own))
    grads = call(finish_kernel, tuple(shape((rows, width), BF16) for _ in range(3)), (own, peer))
    return (grads[0][None], grads[1][None], grads[2][None], weight_grad)


def general_device(queries, keys, values, out_grad, out_weight, slopes, counts, gaps):
    row_count = queries.shape[1]
    width = queries.shape[2]
    head_count = slopes.shape[0]
    head_size = width // head_count
    scaling = head_size ** (-0.5)
    shard_count = lax.axis_size("context")
    my_start = lax.axis_index("context") * row_count
    total_slots = shard_count * row_count
    all_gaps, all_counts = (
        lax.all_gather(gaps, "context", axis=1, tiled=True),
        lax.all_gather(counts, "context", axis=1, tiled=True),
    )
    slot_index = jnp.arange(total_slots, dtype=jnp.int32)
    owner = slot_index // row_count
    shard_ids = jnp.arange(shard_count, dtype=jnp.int32)
    slot_limit = jnp.sum(
        jnp.where(owner[:, None] == shard_ids[None, :], all_counts[0][None, :], 0), axis=1
    )
    slot_valid = slot_index % row_count < slot_limit
    offsets = jnp.cumsum(jnp.where(slot_valid, all_gaps[0], 0)).astype(jnp.float32)
    my_valid = lax.dynamic_slice_in_dim(slot_valid, my_start, row_count)
    grad_full = lax.all_gather(out_grad[0], "tensor", axis=1, tiled=True)
    grad_masked = jnp.where(my_valid[:, None], grad_full, jnp.zeros_like(grad_full))
    columns = grad_masked
    grad_heads = jnp.dot(
        columns,
        lax.all_gather(out_weight, "fsdp", axis=0, tiled=True),
        preferred_element_type=jnp.float32,
    ).astype(jnp.bfloat16)
    local_q = queries[0]
    local_k = keys[0]
    local_v = values[0]
    key_full, value_full = (
        lax.all_gather(local_k, "context", axis=0, tiled=True),
        lax.all_gather(local_v, "context", axis=0, tiled=True),
    )

    def split(block):
        return block.reshape(block.shape[0], head_count, head_size)

    def scores(q_block, q_start, k_block, k_start):
        query_count = q_block.shape[0]
        key_count = k_block.shape[0]
        logits = (
            jnp.einsum(
                "qhd,khd->hqk", split(q_block), split(k_block), preferred_element_type=jnp.float32
            )
            * scaling
        )
        q_offset = lax.dynamic_slice_in_dim(offsets, q_start, query_count)
        k_offset = lax.dynamic_slice_in_dim(offsets, k_start, key_count)
        k_valid = lax.dynamic_slice_in_dim(slot_valid, k_start, key_count)
        q_slot = q_start + jnp.arange(query_count, dtype=jnp.int32)
        k_slot = k_start + jnp.arange(key_count, dtype=jnp.int32)
        allowed = k_valid[None, :] & (k_slot[None, :] <= q_slot[:, None])
        logits = logits - slopes[:, None, None] * (
            q_offset[None, :, None] - k_offset[None, None, :]
        )
        return (jnp.where(allowed[None], logits, NEG), allowed)

    def tile_terms(q_block, g_block, q_lse, q_delta, q_start, k_block, v_block, k_start):
        logits, allowed = scores(q_block, q_start, k_block, k_start)
        probs = jnp.where(allowed[None], jnp.exp(logits - q_lse[:, :, None]), 0.0)
        value_dots = jnp.einsum(
            "qhd,khd->hqk", split(g_block), split(v_block), preferred_element_type=jnp.float32
        )
        dscore = (probs * (value_dots - q_delta[:, :, None])).astype(jnp.bfloat16)
        return (probs.astype(jnp.bfloat16), dscore)

    block = 2 * row_count
    block_total = total_slots // block

    def mass_step(block_index, carry):
        k_start = block_index * block
        k_block = lax.dynamic_slice_in_dim(key_full, k_start, block, 0)

        def work(state):
            peak, mass = state
            logits, allowed = scores(local_q, my_start, k_block, k_start)
            new_peak = jnp.maximum(peak, jnp.max(logits, axis=2))
            weights = jnp.where(allowed[None], jnp.exp(logits - new_peak[:, :, None]), 0.0)
            return (new_peak, mass * jnp.exp(peak - new_peak) + jnp.sum(weights, axis=2))

        return work(carry)

    start_state = (
        jnp.full((head_count, row_count), NEG, jnp.float32),
        jnp.zeros((head_count, row_count), jnp.float32),
    )
    peak, mass = lax.fori_loop(0, block_total, mass_step, start_state)
    log_total = peak + jnp.log(mass)

    def output_step(block_index, carry):
        k_start = block_index * block
        k_block = lax.dynamic_slice_in_dim(key_full, k_start, block, 0)
        v_block = lax.dynamic_slice_in_dim(value_full, k_start, block, 0)

        def work(acc):
            logits, allowed = scores(local_q, my_start, k_block, k_start)
            probs_b = jnp.where(allowed[None], jnp.exp(logits - log_total[:, :, None]), 0.0).astype(
                jnp.bfloat16
            )
            return acc + jnp.einsum(
                "hqk,khd->qhd", probs_b, split(v_block), preferred_element_type=jnp.float32
            ).reshape(row_count, width)

        return work(carry)

    output_b = lax.fori_loop(
        0, block_total, output_step, jnp.zeros((row_count, width), jnp.float32)
    ).astype(jnp.bfloat16)
    delta = jnp.sum(
        (grad_heads.astype(jnp.float32) * output_b.astype(jnp.float32)).reshape(
            row_count, head_count, head_size
        ),
        axis=2,
    ).T

    def query_step(block_index, carry):
        k_start = block_index * block
        k_block = lax.dynamic_slice_in_dim(key_full, k_start, block, 0)
        v_block = lax.dynamic_slice_in_dim(value_full, k_start, block, 0)

        def work(acc):
            probs_b, dscore = tile_terms(
                local_q, grad_heads, log_total, delta, my_start, k_block, v_block, k_start
            )
            return (
                acc
                + jnp.einsum(
                    "hqk,khd->qhd", dscore, split(k_block), preferred_element_type=jnp.float32
                ).reshape(row_count, width)
                * scaling
            )

        return work(carry)

    query_grad = lax.fori_loop(
        0, block_total, query_step, jnp.zeros((row_count, width), jnp.float32)
    ).astype(jnp.bfloat16)
    stats_lse, stats_delta = (
        lax.all_gather(log_total, "context", axis=1, tiled=True),
        lax.all_gather(delta, "context", axis=1, tiled=True),
    )
    start = jnp.int32(0)
    q_piece = lax.all_gather(local_q, "context", axis=0, tiled=True)
    g_piece = lax.all_gather(grad_heads, "context", axis=0, tiled=True)

    def work(held):
        probs_b, dscore = tile_terms(
            q_piece, g_piece, stats_lse, stats_delta, start, local_k, local_v, my_start
        )
        key_part = (
            jnp.einsum(
                "hqk,qhd->khd", dscore, split(q_piece), preferred_element_type=jnp.float32
            ).reshape(row_count, width)
            * scaling
        )
        value_part = jnp.einsum(
            "hqk,qhd->khd", probs_b, split(g_piece), preferred_element_type=jnp.float32
        ).reshape(row_count, width)
        return jnp.concatenate([key_part, value_part], axis=1)

    key_value_grads = work(jnp.zeros((row_count, 2 * width), jnp.float32))
    key_grad = key_value_grads[:, :width].astype(jnp.bfloat16)
    value_grad = key_value_grads[:, width:].astype(jnp.bfloat16)
    columns = grad_masked
    weight_share = lax.psum_scatter(
        lax.dot_general(
            columns, output_b, (((0,), (0,)), ((), ())), preferred_element_type=jnp.float32
        ),
        "fsdp",
        scatter_dimension=0,
        tiled=True,
    )
    weight_grad = lax.psum(weight_share, "context")
    return (query_grad[None], key_grad[None], value_grad[None], weight_grad)


def solution(mesh):
    placed = (
        P("fsdp", "context", "tensor"),
        P("fsdp", "context", "tensor"),
        P("fsdp", "context", "tensor"),
        P("fsdp", "context", "tensor"),
        P("fsdp", "tensor"),
        P("tensor"),
        P("fsdp", "context"),
        P("fsdp", "context"),
    )
    sizes = dict(mesh.shape)
    packs = sizes["context"] == 2 and sizes["tensor"] == 4 and sizes["fsdp"] == 4
    return jax.shard_map(
        packed_device if packs else general_device,
        mesh=mesh,
        in_specs=placed,
        out_specs=(
            P("fsdp", "context", "tensor"),
            P("fsdp", "context", "tensor"),
            P("fsdp", "context", "tensor"),
            P("fsdp", "tensor"),
        ),
        check_vma=False,
    )
```

```python
import functools

import jax
import jax.numpy as jnp
from jax import lax
from jax.experimental import pallas as pl
from jax.experimental.pallas import tpu as pltpu
from jax.sharding import PartitionSpec as P

NEG = -1e30
F32 = jnp.float32
BF16 = jnp.bfloat16
NN = (((1,), (0,)), ((), ()))
NT = (((1,), (1,)), ((), ()))
TN = (((0,), (0,)), ((), ()))


def dot(a, b, dims=NN):
    return lax.dot_general(a, b, dims, preferred_element_type=F32)


def iota(shape, axis):
    return lax.broadcasted_iota(jnp.int32, shape, axis)


def onehot(mask):
    return jnp.where(mask, 1.0, 0.0).astype(BF16)


def call(body, outs, args, smem=(), out=pltpu.VMEM, scratch=(), vmem=8):
    return pl.pallas_call(
        body,
        out_shape=outs,
        in_specs=[
            pl.BlockSpec(memory_space=pltpu.SMEM if i in smem else pltpu.VMEM)
            for i in range(len(args))
        ],
        out_specs=jax.tree.map(lambda _: pl.BlockSpec(memory_space=out), outs),
        scratch_shapes=list(scratch),
        compiler_params=pltpu.CompilerParams(vmem_limit_bytes=vmem * 2**20),
    )(*args)


def packed_slot(index, half, rows, count0, count1):
    own0 = jnp.where(index < count0, index, rows + half + index - count0)
    other = index - half
    own1 = jnp.where(other < count1, rows + other, half + other - count1)
    return jnp.where(index < half, own0, own1)


def pack_rows_kernel(count_ref, own_ref, extra_ref, out_ref):
    half = out_ref.shape[0]
    extra = extra_ref.shape[0]
    count = count_ref[0, 0]
    at, row = iota((half, half), 0), iota((half, half), 1)
    first = onehot((at == row) & (at < count))
    at, row = iota((half, extra), 0), iota((half, extra), 1)
    second = onehot((at >= count) & (at - count == row))
    out_ref[...] = (dot(first, own_ref[...]) + dot(second, extra_ref[...])).astype(BF16)


def forward_kernel(
    count_ref, slopes_ref, mine_ref, message_ref, q_out, k_out, v_out, probs_out, output_ref
):
    part = mine_ref.shape[1]
    rows = (mine_ref.shape[0] - 16) // 3
    total = q_out.shape[0]
    half = total // 2
    heads = probs_out.shape[0]
    size = part // heads
    c = lax.axis_index("context")
    count = count_ref[0, 0]
    count0 = jnp.where(c == 0, count, total - count)
    count1 = total - count0
    slot_down = packed_slot(iota((total, rows), 0), half, rows, count0, count1)
    slot_here = iota((total, rows), 1)
    own_slot = c * rows + slot_here
    peer_slot = (1 - c) * rows + slot_here
    own_pick, peer_pick = onehot(slot_down == own_slot), onehot(slot_down == peer_slot)
    own_until = onehot((own_slot <= slot_down) & (slot_here < count))
    peer_until = onehot((peer_slot <= slot_down) & (slot_here < total - count))
    own_gaps = mine_ref[3 * rows :, :rows]
    peer_gaps = message_ref[3 * rows :, :rows]
    offset_down = (dot(own_until, own_gaps, NT) + dot(peer_until, peer_gaps, NT))[:, :1]
    offset_across = (dot(own_gaps, own_until, NT) + dot(peer_gaps, peer_until, NT))[:1, :]
    slot_q = packed_slot(iota((total, total), 0), half, rows, count0, count1)
    slot_k = packed_slot(iota((total, total), 1), half, rows, count0, count1)
    allowed = slot_k <= slot_q
    distance = offset_down - offset_across
    for n, out in enumerate((q_out, k_out, v_out)):
        at = slice(n * rows, (n + 1) * rows)
        out[...] = (dot(own_pick, mine_ref[at, :]) + dot(peer_pick, message_ref[at, :])).astype(BF16)
    for h in range(heads):
        cols = slice(h * size, (h + 1) * size)
        slope = slopes_ref[c * heads + h]
        score = dot(q_out[:, cols], k_out[:, cols], NT) * (size**-0.5) - slope * distance
        score = jnp.where(allowed, score, NEG)
        peak = jnp.max(score, axis=1, keepdims=True)
        mass = jnp.where(allowed, jnp.exp(score - peak), 0.0)
        probs = mass / jnp.sum(mass, axis=1, keepdims=True)
        probs_out[h] = probs
        output_ref[:, cols] = dot(probs.astype(BF16), v_out[:, cols]).astype(BF16)


def place(blocks, own_ref, near_ref):
    half = own_ref.shape[0] // 2
    t, f = lax.axis_index("tensor"), lax.axis_index("fsdp")
    h, l, x, core = t // 2, t % 2, f // 2, f % 2
    swap_seq = (h + x) % 2
    swap_chunk = (l + core) % 2
    for seq in range(2):
        for chunk in range(2):

            @pl.when((swap_seq == seq) & (swap_chunk == chunk))
            def _(seq=seq, chunk=chunk):
                for n in range(2):
                    at = slice(n * half, (n + 1) * half)
                    own_ref[at, :] = blocks[n ^ seq][chunk][...]
                    near_ref[at, :] = blocks[n ^ seq][1 - chunk][...]


def bundle_kernel(
    p00_ref, p01_ref, p10_ref, p11_ref, mine_ref, mine_x_ref, away_ref, away_x_ref,
    own_p_ref, bundle_ref,
):
    pair, part = mine_ref.shape
    blocks = (p00_ref, p01_ref), (p10_ref, p11_ref)
    place(blocks, own_p_ref, bundle_ref.at[:pair])
    bundle_ref[pair : 2 * pair, :part] = mine_ref[...]
    bundle_ref[pair : 2 * pair, part:] = mine_x_ref[...]
    bundle_ref[2 * pair :, :part] = away_ref[...]
    bundle_ref[2 * pair :, part:] = away_x_ref[...]


def partial_kernel(
    b00_ref, b01_ref, b10_ref, b11_ref, own_w_ref, near_w_ref,
    keep_ref, send_x_ref, send_y_ref, send_xy_ref, own_g_ref, near_g_ref, total_ref,
):
    half, part = keep_ref.shape
    place(((b00_ref, b01_ref), (b10_ref, b11_ref)), own_g_ref, near_g_ref)
    total_ref[...] = dot(own_g_ref[...], own_w_ref[...]) + dot(near_g_ref[...], near_w_ref[...])
    c = lax.axis_index("context")
    mine = pl.ds(pl.multiple_of(c * part, part), part)
    away = pl.ds(pl.multiple_of((1 - c) * part, part), part)
    keep_ref[...] = total_ref[:half, mine]
    send_x_ref[...] = total_ref[half:, mine].astype(BF16)
    send_y_ref[...] = total_ref[:half, away].astype(BF16)
    send_xy_ref[...] = total_ref[half:, away].astype(BF16)


def backward_kernel(
    count_ref, q_ref, k_ref, v_ref, probs_ref, output_ref, keep_ref, from_x_ref, from_y_ref, from_xy_ref,
    own_ref, send_ref, send_q_ref, g_ref, grads_ref,
):
    total, part = q_ref.shape
    half = total // 2
    heads = probs_ref.shape[0]
    size = part // heads
    rows = own_ref.shape[0] // 3
    c = lax.axis_index("context")
    count = count_ref[0, 0]
    count0 = jnp.where(c == 0, count, total - count)
    here = (keep_ref[...] + from_x_ref[...].astype(F32)).astype(BF16)
    there = (from_y_ref[...].astype(F32) + from_xy_ref[...].astype(F32)).astype(BF16)
    g_ref[pl.ds(pl.multiple_of(c * half, half), half), :] = here
    g_ref[pl.ds(pl.multiple_of((1 - c) * half, half), half), :] = there
    for h in range(heads):
        cols = slice(h * size, (h + 1) * size)
        probs = probs_ref[h]
        g, q, k, v = g_ref[:, cols], q_ref[:, cols], k_ref[:, cols], v_ref[:, cols]
        delta = jnp.sum(g.astype(F32) * output_ref[:, cols].astype(F32), axis=1, keepdims=True)
        dscore = (probs * (dot(g, v, NT) - delta)).astype(BF16)
        grads_ref[0, :, cols] = (dot(dscore, k) * (size**-0.5)).astype(BF16)
        grads_ref[1, :, cols] = (dot(dscore, q, TN) * (size**-0.5)).astype(BF16)
        grads_ref[2, :, cols] = dot(probs.astype(BF16), g, TN).astype(BF16)
    slot = packed_slot(iota((rows, total), 1), half, rows, count0, total - count0)
    row = iota((rows, total), 0)
    own_pick, peer_pick = onehot(slot == c * rows + row), onehot(slot == (1 - c) * rows + row)
    send_q_ref[...] = dot(peer_pick, grads_ref[0]).astype(BF16)
    for n in range(1, 3):
        send_ref[(n - 1) * rows : n * rows, :] = dot(peer_pick, grads_ref[n]).astype(BF16)
    for n in range(3):
        own_ref[n * rows : (n + 1) * rows, :] = dot(own_pick, grads_ref[n]).astype(BF16)


def finish_kernel(own_ref, peer_ref, peer_q_ref, q_ref, k_ref, v_ref, sems):
    rows, width = q_ref.shape
    part = width // 2
    c = lax.axis_index("context")
    copies = []
    own = [own_ref.at[n * rows : (n + 1) * rows, :] for n in range(3)]
    peer = [peer_q_ref, peer_ref.at[:rows, :], peer_ref.at[rows:, :]]
    for side, sources in enumerate((own, peer)):
        at = pl.ds(pl.multiple_of((c if side == 0 else 1 - c) * part, part), part)
        for n, ref in enumerate((q_ref, k_ref, v_ref)):
            copies.append(pltpu.make_async_copy(sources[n], ref.at[:, at], sems.at[side, n]))
    for copy in copies:
        copy.start()
    for copy in copies:
        copy.wait()


def weight_kernel(
    own_g_ref, near_g_ref, own_p_ref, bundle_ref, mine_ref, mine_x_ref, away_ref, away_x_ref,
    weight_ref, left_ref, right_ref, done_ref, sems,
):
    pair, width = own_g_ref.shape
    half, part = pair // 2, width // 2
    blocks, block = done_ref.shape[:2]
    c = lax.axis_index("context")
    pieces = (own_g_ref, near_g_ref), (own_p_ref, bundle_ref.at[:pair])
    for which, refs in enumerate(pieces):
        for n, ref in enumerate(refs):
            for s in range(2):
                row = (2 * n + s) * pair + (c if which == 0 else 1 - c) * half
                left_ref[pl.ds(pl.multiple_of(row, half), half), :] = ref[
                    s * half : (s + 1) * half, :
                ]
    sides = (mine_ref, mine_x_ref), (away_ref, away_x_ref)
    for side, refs in enumerate(sides):
        at = pl.ds(pl.multiple_of((c if side == 0 else 1 - c) * part, part), part)
        near = (side + 1) * pair
        for s in range(2):
            cols = slice(s * part, (s + 1) * part)
            right_ref[s * pair : (s + 1) * pair, at] = refs[s][...]
            right_ref[(s + 2) * pair : (s + 3) * pair, at] = bundle_ref[near : near + pair, cols]
    copies = []
    for n in range(blocks):
        rows = slice(n * block, (n + 1) * block)
        done_ref[n] = dot(left_ref[:, rows], right_ref[...], TN)
        copies.append(pltpu.make_async_copy(done_ref.at[n], weight_ref.at[rows, :], sems.at[n]))
        copies[-1].start()
    for copy in copies:
        copy.wait()


def spread(flip):
    pairs = []
    for t in range(4):
        for f in range(4):
            h, l, x, core = t >> 1, t & 1, f >> 1, f & 1
            pairs.append((t * 4 + f, ((x ^ flip) << 1 | l) * 4 + (h << 1 | core)))
    return pairs


def packed_device(queries, keys, values, out_grad, out_weight, slopes, counts, gaps):
    rows, width = queries.shape[1:]
    part = width // 2
    total = 2 * rows * 5 // 8
    half = total // 2
    heads = slopes.shape[0] // 2
    shape = jax.ShapeDtypeStruct
    over_y = lambda a: lax.ppermute(a, "context", [(0, 1), (1, 0)])
    over_x = lambda a: lax.ppermute(a, "fsdp", [(i, i ^ 2) for i in range(4)])
    over_core = lambda a: lax.ppermute(a, "fsdp", [(i, i ^ 1) for i in range(4)])
    after = lax.optimization_barrier

    grad = out_grad[0]
    c = lax.axis_index("context")

    def side(which, q, k, v):
        cut = lambda a: lax.dynamic_slice_in_dim(a[0], which * part, part, 1)
        return jnp.concatenate([cut(q), cut(k), cut(v), tail], axis=0)

    extra, gaps, near_weight, *source = after(
        (grad[half:], gaps, out_weight, queries, keys, values)
    )
    near_weight = over_core(near_weight)
    extra = over_y(extra)
    tail = jnp.broadcast_to(gaps.astype(BF16), (16, rows))
    tail = jnp.concatenate([tail] * (part // rows), axis=1)
    message = side(1 - c, *source)
    packed = call(
        pack_rows_kernel, shape((half, width), BF16), (counts, grad[:half], extra), smem=(0,)
    )
    message = over_y(message)
    packed, near_weight, *source = after((packed, near_weight, *source))
    mine = side(c, *source)
    first, second = [lax.ppermute(packed, ("tensor", "fsdp"), spread(a)) for a in (0, 1)]
    over_z = lambda a: lax.ppermute(a, "tensor", [(i, i ^ 1) for i in range(4)])
    blocks = [first, over_z(first), second, over_z(second)]
    q, k, v, probs, output = call(
        forward_kernel,
        (
            shape((total, part), BF16),
            shape((total, part), BF16),
            shape((total, part), BF16),
            shape((heads, total, total), F32),
            shape((total, part), BF16),
        ),
        (counts, slopes, mine, message),
        smem=(0, 1),
    )
    out_x = over_x(output)
    peer_output = over_y(output)
    peer_first, peer_second = over_y(first), over_y(second)
    peer_first_z = over_z(peer_first)
    *blocks, output, peer_first, peer_second = after((*blocks, output, peer_first, peer_second))
    keep, send_x, send_y, send_xy, own_g, near_g = call(
        partial_kernel,
        (
            shape((half, part), F32),
            shape((half, part), BF16),
            shape((half, part), BF16),
            shape((half, part), BF16),
            shape((total, width), BF16),
            shape((total, width), BF16),
        ),
        (*blocks, out_weight, near_weight),
        scratch=(pltpu.VMEM((total, width), F32),),
    )
    from_xy = lax.ppermute(
        send_xy,
        ("context", "fsdp"),
        [(c * 4 + f, (1 - c) * 4 + (f ^ 2)) for c in range(2) for f in range(4)],
    )
    from_x, from_y = over_x(send_x), over_y(send_y)
    from_x, from_y, from_xy, peer_output = after((from_x, from_y, from_xy, peer_output))
    own, send, send_q = call(
        backward_kernel,
        (
            shape((3 * rows, part), BF16),
            shape((2 * rows, part), BF16),
            shape((rows, part), BF16),
        ),
        (counts, q, k, v, probs, output, keep, from_x, from_y, from_xy),
        smem=(0,),
        scratch=(pltpu.VMEM((total, part), BF16), pltpu.VMEM((3, total, part), BF16)),
    )
    peer = over_y(send)
    near_g, peer_second, peer_output = after((near_g, peer_second, peer_output, send))[:3]
    near_g = over_core(near_g)
    peer_second_z = over_z(peer_second)
    peer_x = over_x(peer_output)
    bundled = (
        peer_first, peer_first_z, peer_second, peer_second_z, output, out_x, peer_output, peer_x
    )
    *bundled, peer, send_q = after((*bundled, peer, send_q))
    peer_q = over_y(send_q)
    own_p, bundle = call(
        bundle_kernel,
        (shape((total, width), BF16), shape((3 * total, width), BF16)),
        bundled,
    )
    bundle = over_core(bundle)
    weight_grad = call(
        weight_kernel,
        shape(out_weight.shape, F32),
        (own_g, near_g, own_p, bundle, output, out_x, peer_output, peer_x),
        out=pl.ANY,
        scratch=(
            pltpu.VMEM((4 * total, width), BF16),
            pltpu.VMEM((4 * total, width), BF16),
            pltpu.VMEM((4, width // 4, width), F32),
            pltpu.SemaphoreType.DMA((4,)),
        ),
        vmem=16,
    )
    weight_grad, own = after((weight_grad, own))
    grads = call(
        finish_kernel,
        tuple(shape((rows, width), BF16) for _ in range(3)),
        (own, peer, peer_q),
        out=pl.ANY,
        scratch=(pltpu.SemaphoreType.DMA((2, 3)),),
    )
    return (grads[0][None], grads[1][None], grads[2][None], weight_grad)


def general_device(queries, keys, values, out_grad, out_weight, slopes, counts, gaps):
    row_count = queries.shape[1]
    width = queries.shape[2]
    head_count = slopes.shape[0]
    head_size = width // head_count
    scaling = head_size ** (-0.5)
    shard_count = lax.axis_size("context")
    my_start = lax.axis_index("context") * row_count
    total_slots = shard_count * row_count
    all_gaps, all_counts = (
        lax.all_gather(gaps, "context", axis=1, tiled=True),
        lax.all_gather(counts, "context", axis=1, tiled=True),
    )
    slot_index = jnp.arange(total_slots, dtype=jnp.int32)
    owner = slot_index // row_count
    shard_ids = jnp.arange(shard_count, dtype=jnp.int32)
    slot_limit = jnp.sum(
        jnp.where(owner[:, None] == shard_ids[None, :], all_counts[0][None, :], 0), axis=1
    )
    slot_valid = slot_index % row_count < slot_limit
    offsets = jnp.cumsum(jnp.where(slot_valid, all_gaps[0], 0)).astype(jnp.float32)
    my_valid = lax.dynamic_slice_in_dim(slot_valid, my_start, row_count)
    grad_full = lax.all_gather(out_grad[0], "tensor", axis=1, tiled=True)
    grad_masked = jnp.where(my_valid[:, None], grad_full, jnp.zeros_like(grad_full))
    columns = grad_masked
    grad_heads = jnp.dot(
        columns,
        lax.all_gather(out_weight, "fsdp", axis=0, tiled=True),
        preferred_element_type=jnp.float32,
    ).astype(jnp.bfloat16)
    local_q = queries[0]
    local_k = keys[0]
    local_v = values[0]
    key_full, value_full = (
        lax.all_gather(local_k, "context", axis=0, tiled=True),
        lax.all_gather(local_v, "context", axis=0, tiled=True),
    )

    def split(block):
        return block.reshape(block.shape[0], head_count, head_size)

    def scores(q_block, q_start, k_block, k_start):
        query_count = q_block.shape[0]
        key_count = k_block.shape[0]
        logits = (
            jnp.einsum(
                "qhd,khd->hqk", split(q_block), split(k_block), preferred_element_type=jnp.float32
            )
            * scaling
        )
        q_offset = lax.dynamic_slice_in_dim(offsets, q_start, query_count)
        k_offset = lax.dynamic_slice_in_dim(offsets, k_start, key_count)
        k_valid = lax.dynamic_slice_in_dim(slot_valid, k_start, key_count)
        q_slot = q_start + jnp.arange(query_count, dtype=jnp.int32)
        k_slot = k_start + jnp.arange(key_count, dtype=jnp.int32)
        allowed = k_valid[None, :] & (k_slot[None, :] <= q_slot[:, None])
        logits = logits - slopes[:, None, None] * (
            q_offset[None, :, None] - k_offset[None, None, :]
        )
        return (jnp.where(allowed[None], logits, NEG), allowed)

    def tile_terms(q_block, g_block, q_lse, q_delta, q_start, k_block, v_block, k_start):
        logits, allowed = scores(q_block, q_start, k_block, k_start)
        probs = jnp.where(allowed[None], jnp.exp(logits - q_lse[:, :, None]), 0.0)
        value_dots = jnp.einsum(
            "qhd,khd->hqk", split(g_block), split(v_block), preferred_element_type=jnp.float32
        )
        dscore = (probs * (value_dots - q_delta[:, :, None])).astype(jnp.bfloat16)
        return (probs.astype(jnp.bfloat16), dscore)

    block = 2 * row_count
    block_total = total_slots // block

    def mass_step(block_index, carry):
        k_start = block_index * block
        k_block = lax.dynamic_slice_in_dim(key_full, k_start, block, 0)

        def work(state):
            peak, mass = state
            logits, allowed = scores(local_q, my_start, k_block, k_start)
            new_peak = jnp.maximum(peak, jnp.max(logits, axis=2))
            weights = jnp.where(allowed[None], jnp.exp(logits - new_peak[:, :, None]), 0.0)
            return (new_peak, mass * jnp.exp(peak - new_peak) + jnp.sum(weights, axis=2))

        return work(carry)

    start_state = (
        jnp.full((head_count, row_count), NEG, jnp.float32),
        jnp.zeros((head_count, row_count), jnp.float32),
    )
    peak, mass = lax.fori_loop(0, block_total, mass_step, start_state)
    log_total = peak + jnp.log(mass)

    def output_step(block_index, carry):
        k_start = block_index * block
        k_block = lax.dynamic_slice_in_dim(key_full, k_start, block, 0)
        v_block = lax.dynamic_slice_in_dim(value_full, k_start, block, 0)

        def work(acc):
            logits, allowed = scores(local_q, my_start, k_block, k_start)
            probs_b = jnp.where(allowed[None], jnp.exp(logits - log_total[:, :, None]), 0.0).astype(
                jnp.bfloat16
            )
            return acc + jnp.einsum(
                "hqk,khd->qhd", probs_b, split(v_block), preferred_element_type=jnp.float32
            ).reshape(row_count, width)

        return work(carry)

    output_b = lax.fori_loop(
        0, block_total, output_step, jnp.zeros((row_count, width), jnp.float32)
    ).astype(jnp.bfloat16)
    delta = jnp.sum(
        (grad_heads.astype(jnp.float32) * output_b.astype(jnp.float32)).reshape(
            row_count, head_count, head_size
        ),
        axis=2,
    ).T

    def query_step(block_index, carry):
        k_start = block_index * block
        k_block = lax.dynamic_slice_in_dim(key_full, k_start, block, 0)
        v_block = lax.dynamic_slice_in_dim(value_full, k_start, block, 0)

        def work(acc):
            probs_b, dscore = tile_terms(
                local_q, grad_heads, log_total, delta, my_start, k_block, v_block, k_start
            )
            return (
                acc
                + jnp.einsum(
                    "hqk,khd->qhd", dscore, split(k_block), preferred_element_type=jnp.float32
                ).reshape(row_count, width)
                * scaling
            )

        return work(carry)

    query_grad = lax.fori_loop(
        0, block_total, query_step, jnp.zeros((row_count, width), jnp.float32)
    ).astype(jnp.bfloat16)
    stats_lse, stats_delta = (
        lax.all_gather(log_total, "context", axis=1, tiled=True),
        lax.all_gather(delta, "context", axis=1, tiled=True),
    )
    start = jnp.int32(0)
    q_piece = lax.all_gather(local_q, "context", axis=0, tiled=True)
    g_piece = lax.all_gather(grad_heads, "context", axis=0, tiled=True)

    def work(held):
        probs_b, dscore = tile_terms(
            q_piece, g_piece, stats_lse, stats_delta, start, local_k, local_v, my_start
        )
        key_part = (
            jnp.einsum(
                "hqk,qhd->khd", dscore, split(q_piece), preferred_element_type=jnp.float32
            ).reshape(row_count, width)
            * scaling
        )
        value_part = jnp.einsum(
            "hqk,qhd->khd", probs_b, split(g_piece), preferred_element_type=jnp.float32
        ).reshape(row_count, width)
        return jnp.concatenate([key_part, value_part], axis=1)

    key_value_grads = work(jnp.zeros((row_count, 2 * width), jnp.float32))
    key_grad = key_value_grads[:, :width].astype(jnp.bfloat16)
    value_grad = key_value_grads[:, width:].astype(jnp.bfloat16)
    columns = grad_masked
    weight_share = lax.psum_scatter(
        lax.dot_general(
            columns, output_b, (((0,), (0,)), ((), ())), preferred_element_type=jnp.float32
        ),
        "fsdp",
        scatter_dimension=0,
        tiled=True,
    )
    weight_grad = lax.psum(weight_share, "context")
    return (query_grad[None], key_grad[None], value_grad[None], weight_grad)


def solution(mesh):
    placed = (
        P("fsdp", "context", "tensor"),
        P("fsdp", "context", "tensor"),
        P("fsdp", "context", "tensor"),
        P("fsdp", "context", "tensor"),
        P("fsdp", "tensor"),
        P("tensor"),
        P("fsdp", "context"),
        P("fsdp", "context"),
    )
    sizes = dict(mesh.shape)
    packs = sizes["context"] == 2 and sizes["tensor"] == 4 and sizes["fsdp"] == 4
    return jax.shard_map(
        packed_device if packs else general_device,
        mesh=mesh,
        in_specs=placed,
        out_specs=(
            P("fsdp", "context", "tensor"),
            P("fsdp", "context", "tensor"),
            P("fsdp", "context", "tensor"),
            P("fsdp", "tensor"),
        ),
        check_vma=False,
    )
```

```python
import functools

import jax
import jax.numpy as jnp
from jax import lax
from jax.experimental import pallas as pl
from jax.experimental.pallas import tpu as pltpu
from jax.sharding import PartitionSpec as P

NEG = -1e30
F32 = jnp.float32
BF16 = jnp.bfloat16
NN = (((1,), (0,)), ((), ()))
NT = (((1,), (1,)), ((), ()))
TN = (((0,), (0,)), ((), ()))


def dot(a, b, dims=NN):
    return lax.dot_general(a, b, dims, preferred_element_type=F32)


def iota(shape, axis):
    return lax.broadcasted_iota(jnp.int32, shape, axis)


def onehot(mask):
    return jnp.where(mask, 1.0, 0.0).astype(BF16)


def call(body, outs, args, smem=(), out=pltpu.VMEM, scratch=(), vmem=8):
    return pl.pallas_call(
        body,
        out_shape=outs,
        in_specs=[
            pl.BlockSpec(memory_space=pltpu.SMEM if i in smem else pltpu.VMEM)
            for i in range(len(args))
        ],
        out_specs=jax.tree.map(lambda _: pl.BlockSpec(memory_space=out), outs),
        scratch_shapes=list(scratch),
        compiler_params=pltpu.CompilerParams(vmem_limit_bytes=vmem * 2**20),
    )(*args)


def packed_slot(index, half, rows, count0, count1):
    own0 = jnp.where(index < count0, index, rows + half + index - count0)
    other = index - half
    own1 = jnp.where(other < count1, rows + other, half + other - count1)
    return jnp.where(index < half, own0, own1)


def pack_rows_kernel(count_ref, own_ref, extra_ref, out_ref):
    half = out_ref.shape[0]
    extra = extra_ref.shape[0]
    count = count_ref[0, 0]
    at, row = iota((half, half), 0), iota((half, half), 1)
    first = onehot((at == row) & (at < count))
    at, row = iota((half, extra), 0), iota((half, extra), 1)
    second = onehot((at >= count) & (at - count == row))
    out_ref[...] = (dot(first, own_ref[...]) + dot(second, extra_ref[...])).astype(BF16)


def forward_kernel(
    count_ref, slopes_ref, mine_ref, message_ref, q_out, k_out, v_out, probs_out, output_ref
):
    part = mine_ref.shape[1]
    rows = (mine_ref.shape[0] - 16) // 3
    total = q_out.shape[0]
    half = total // 2
    heads = probs_out.shape[0]
    size = part // heads
    c = lax.axis_index("context")
    count = count_ref[0, 0]
    count0 = jnp.where(c == 0, count, total - count)
    count1 = total - count0
    slot_down = packed_slot(iota((total, rows), 0), half, rows, count0, count1)
    slot_here = iota((total, rows), 1)
    own_slot = c * rows + slot_here
    peer_slot = (1 - c) * rows + slot_here
    own_pick, peer_pick = onehot(slot_down == own_slot), onehot(slot_down == peer_slot)
    own_until = onehot((own_slot <= slot_down) & (slot_here < count))
    peer_until = onehot((peer_slot <= slot_down) & (slot_here < total - count))
    own_gaps = mine_ref[3 * rows :, :rows]
    peer_gaps = message_ref[3 * rows :, :rows]
    offset_down = (dot(own_until, own_gaps, NT) + dot(peer_until, peer_gaps, NT))[:, :1]
    offset_across = (dot(own_gaps, own_until, NT) + dot(peer_gaps, peer_until, NT))[:1, :]
    slot_q = packed_slot(iota((total, total), 0), half, rows, count0, count1)
    slot_k = packed_slot(iota((total, total), 1), half, rows, count0, count1)
    allowed = slot_k <= slot_q
    distance = offset_down - offset_across
    for n, out in enumerate((q_out, k_out, v_out)):
        at = slice(n * rows, (n + 1) * rows)
        out[...] = (dot(own_pick, mine_ref[at, :]) + dot(peer_pick, message_ref[at, :])).astype(BF16)
    for h in range(heads):
        cols = slice(h * size, (h + 1) * size)
        slope = slopes_ref[c * heads + h]
        score = dot(q_out[:, cols], k_out[:, cols], NT) * (size**-0.5) - slope * distance
        score = jnp.where(allowed, score, NEG)
        peak = jnp.max(score, axis=1, keepdims=True)
        mass = jnp.where(allowed, jnp.exp(score - peak), 0.0)
        probs = mass / jnp.sum(mass, axis=1, keepdims=True)
        probs_out[h] = probs
        output_ref[:, cols] = dot(probs.astype(BF16), v_out[:, cols]).astype(BF16)


def place(blocks, own_ref, near_ref):
    half = own_ref.shape[0] // 2
    t, f = lax.axis_index("tensor"), lax.axis_index("fsdp")
    h, l, x, core = t // 2, t % 2, f // 2, f % 2
    swap_seq = (h + x) % 2
    swap_chunk = (l + core) % 2
    for seq in range(2):
        for chunk in range(2):

            @pl.when((swap_seq == seq) & (swap_chunk == chunk))
            def _(seq=seq, chunk=chunk):
                for n in range(2):
                    at = slice(n * half, (n + 1) * half)
                    own_ref[at, :] = blocks[n ^ seq][chunk][...]
                    near_ref[at, :] = blocks[n ^ seq][1 - chunk][...]


def bundle_kernel(
    p00_ref, p01_ref, p10_ref, p11_ref, mine_ref, mine_x_ref, away_ref, away_x_ref,
    own_p_ref, bundle_ref,
):
    pair, part = mine_ref.shape
    blocks = (p00_ref, p01_ref), (p10_ref, p11_ref)
    place(blocks, own_p_ref, bundle_ref.at[:pair])
    bundle_ref[pair : 2 * pair, :part] = mine_ref[...]
    bundle_ref[pair : 2 * pair, part:] = mine_x_ref[...]
    bundle_ref[2 * pair :, :part] = away_ref[...]
    bundle_ref[2 * pair :, part:] = away_x_ref[...]


def partial_kernel(
    b00_ref, b01_ref, b10_ref, b11_ref, own_w_ref, near_w_ref,
    keep_ref, send_x_ref, send_y_ref, send_xy_ref, own_g_ref, near_g_ref, total_ref,
):
    half, part = keep_ref.shape
    place(((b00_ref, b01_ref), (b10_ref, b11_ref)), own_g_ref, near_g_ref)
    total_ref[...] = dot(own_g_ref[...], own_w_ref[...]) + dot(near_g_ref[...], near_w_ref[...])
    c = lax.axis_index("context")
    mine = pl.ds(pl.multiple_of(c * part, part), part)
    away = pl.ds(pl.multiple_of((1 - c) * part, part), part)
    keep_ref[...] = total_ref[:half, mine]
    send_x_ref[...] = total_ref[half:, mine].astype(BF16)
    send_y_ref[...] = total_ref[:half, away].astype(BF16)
    send_xy_ref[...] = total_ref[half:, away].astype(BF16)


def backward_kernel(
    count_ref, q_ref, k_ref, v_ref, probs_ref, output_ref, keep_ref, from_x_ref, from_y_ref, from_xy_ref,
    own_ref, send_ref, send_q_ref, g_ref, grads_ref,
):
    total, part = q_ref.shape
    half = total // 2
    heads = probs_ref.shape[0]
    size = part // heads
    rows = own_ref.shape[0] // 3
    c = lax.axis_index("context")
    count = count_ref[0, 0]
    count0 = jnp.where(c == 0, count, total - count)
    here = (keep_ref[...] + from_x_ref[...].astype(F32)).astype(BF16)
    there = (from_y_ref[...].astype(F32) + from_xy_ref[...].astype(F32)).astype(BF16)
    g_ref[pl.ds(pl.multiple_of(c * half, half), half), :] = here
    g_ref[pl.ds(pl.multiple_of((1 - c) * half, half), half), :] = there
    for h in range(heads):
        cols = slice(h * size, (h + 1) * size)
        probs = probs_ref[h]
        g, q, k, v = g_ref[:, cols], q_ref[:, cols], k_ref[:, cols], v_ref[:, cols]
        delta = jnp.sum(g.astype(F32) * output_ref[:, cols].astype(F32), axis=1, keepdims=True)
        dscore = (probs * (dot(g, v, NT) - delta)).astype(BF16)
        grads_ref[0, :, cols] = (dot(dscore, k) * (size**-0.5)).astype(BF16)
        grads_ref[1, :, cols] = (dot(dscore, q, TN) * (size**-0.5)).astype(BF16)
        grads_ref[2, :, cols] = dot(probs.astype(BF16), g, TN).astype(BF16)
    slot = packed_slot(iota((rows, total), 1), half, rows, count0, total - count0)
    row = iota((rows, total), 0)
    own_pick, peer_pick = onehot(slot == c * rows + row), onehot(slot == (1 - c) * rows + row)
    cut = send_q_ref.shape[0]
    picked = dot(peer_pick, grads_ref[0]).astype(BF16)
    send_q_ref[...] = picked[:cut]
    send_ref[2 * rows :, :] = picked[cut:]
    for n in range(1, 3):
        send_ref[(n - 1) * rows : n * rows, :] = dot(peer_pick, grads_ref[n]).astype(BF16)
    for n in range(3):
        own_ref[n * rows : (n + 1) * rows, :] = dot(own_pick, grads_ref[n]).astype(BF16)


def finish_kernel(own_ref, peer_ref, peer_q_ref, q_ref, k_ref, v_ref, sems):
    rows, width = q_ref.shape
    part = width // 2
    c = lax.axis_index("context")
    copies = []
    own = [own_ref.at[n * rows : (n + 1) * rows, :] for n in range(3)]
    cut = peer_q_ref.shape[0]
    peer = [peer_q_ref, peer_ref.at[:rows, :], peer_ref.at[rows : 2 * rows, :]]
    for side, sources in enumerate((own, peer)):
        at = pl.ds(pl.multiple_of((c if side == 0 else 1 - c) * part, part), part)
        for n, ref in enumerate((q_ref, k_ref, v_ref)):
            to = ref.at[:cut, at] if side == 1 and n == 0 else ref.at[:, at]
            copies.append(pltpu.make_async_copy(sources[n], to, sems.at[side, n]))
    rest = q_ref.at[cut:, pl.ds(pl.multiple_of((1 - c) * part, part), part)]
    copies.append(pltpu.make_async_copy(peer_ref.at[2 * rows :, :], rest, sems.at[2, 0]))
    for copy in copies:
        copy.start()
    for copy in copies:
        copy.wait()


def weight_operands(grads, outputs, left_ref, right_ref):
    pair = grads[0].shape[0]
    half, part = pair // 2, right_ref.shape[1] // 2
    c = lax.axis_index("context")
    for which, ref in enumerate(grads):
        for s in range(2):
            row = s * pair + (c if which == 0 else 1 - c) * half
            left_ref[pl.ds(pl.multiple_of(row, half), half), :] = ref[s * half : (s + 1) * half, :]
    for side, refs in enumerate(outputs):
        at = pl.ds(pl.multiple_of((c if side == 0 else 1 - c) * part, part), part)
        for s, ref in enumerate(refs):
            right_ref[s * pair : (s + 1) * pair, at] = ref[...]


def own_weight_kernel(
    own_g_ref, own_p_ref, mine_ref, mine_x_ref, away_ref, away_x_ref,
    total_ref, left_ref, right_ref,
):
    outputs = (mine_ref, mine_x_ref), (away_ref, away_x_ref)
    weight_operands((own_g_ref, own_p_ref), outputs, left_ref, right_ref)
    block = left_ref.shape[1] // 4
    for n in range(4):
        rows = slice(n * block, (n + 1) * block)
        total_ref[rows, :] = dot(left_ref[:, rows], right_ref[...], TN).astype(BF16)


def weight_kernel(
    total_ref, near_g_ref, bundle_ref, weight_ref, left_ref, right_ref, done_ref, sems
):
    pair, part = near_g_ref.shape[0], near_g_ref.shape[1] // 2
    outputs = [
        [bundle_ref.at[n * pair : (n + 1) * pair, s * part : (s + 1) * part] for s in range(2)]
        for n in (1, 2)
    ]
    weight_operands((near_g_ref, bundle_ref.at[:pair]), outputs, left_ref, right_ref)
    blocks, block = done_ref.shape[:2]
    copies = []
    for n in range(blocks):
        rows = slice(n * block, (n + 1) * block)
        done_ref[n] = total_ref[rows, :].astype(F32) + dot(left_ref[:, rows], right_ref[...], TN)
        copies.append(pltpu.make_async_copy(done_ref.at[n], weight_ref.at[rows, :], sems.at[n]))
        copies[-1].start()
    for copy in copies:
        copy.wait()


def spread(flip):
    pairs = []
    for t in range(4):
        for f in range(4):
            h, l, x, core = t >> 1, t & 1, f >> 1, f & 1
            pairs.append((t * 4 + f, ((x ^ flip) << 1 | l) * 4 + (h << 1 | core)))
    return pairs


def packed_device(queries, keys, values, out_grad, out_weight, slopes, counts, gaps):
    rows, width = queries.shape[1:]
    part = width // 2
    total = 2 * rows * 5 // 8
    half = total // 2
    heads = slopes.shape[0] // 2
    shape = jax.ShapeDtypeStruct
    over_y = lambda a: lax.ppermute(a, "context", [(0, 1), (1, 0)])
    over_x = lambda a: lax.ppermute(a, "fsdp", [(i, i ^ 2) for i in range(4)])
    over_core = lambda a: lax.ppermute(a, "fsdp", [(i, i ^ 1) for i in range(4)])
    after = lax.optimization_barrier

    grad = out_grad[0]
    c = lax.axis_index("context")

    def side(which, q, k, v):
        cut = lambda a: lax.dynamic_slice_in_dim(a[0], which * part, part, 1)
        return jnp.concatenate([cut(q), cut(k), cut(v), tail], axis=0)

    extra, gaps, near_weight, *source = after(
        (grad[half:], gaps, out_weight, queries, keys, values)
    )
    near_weight = over_core(near_weight)
    extra = over_y(extra)
    tail = jnp.broadcast_to(gaps.astype(BF16), (16, rows))
    tail = jnp.concatenate([tail] * (part // rows), axis=1)
    message = side(1 - c, *source)
    packed = call(
        pack_rows_kernel, shape((half, width), BF16), (counts, grad[:half], extra), smem=(0,)
    )
    message = over_y(message)
    packed, near_weight, *source = after((packed, near_weight, *source))
    mine = side(c, *source)
    first, second = [lax.ppermute(packed, ("tensor", "fsdp"), spread(a)) for a in (0, 1)]
    over_z = lambda a: lax.ppermute(a, "tensor", [(i, i ^ 1) for i in range(4)])
    blocks = [first, over_z(first), second, over_z(second)]
    q, k, v, probs, output = call(
        forward_kernel,
        (
            shape((total, part), BF16),
            shape((total, part), BF16),
            shape((total, part), BF16),
            shape((heads, total, total), F32),
            shape((total, part), BF16),
        ),
        (counts, slopes, mine, message),
        smem=(0, 1),
    )
    out_x = over_x(output)
    peer_output = over_y(output)
    peer_first, peer_second = over_y(first), over_y(second)
    peer_first_z = over_z(peer_first)
    *blocks, output, peer_first, peer_second = after((*blocks, output, peer_first, peer_second))
    keep, send_x, send_y, send_xy, own_g, near_g = call(
        partial_kernel,
        (
            shape((half, part), F32),
            shape((half, part), BF16),
            shape((half, part), BF16),
            shape((half, part), BF16),
            shape((total, width), BF16),
            shape((total, width), BF16),
        ),
        (*blocks, out_weight, near_weight),
        scratch=(pltpu.VMEM((total, width), F32),),
    )
    from_xy = lax.ppermute(
        send_xy,
        ("context", "fsdp"),
        [(c * 4 + f, (1 - c) * 4 + (f ^ 2)) for c in range(2) for f in range(4)],
    )
    from_x, from_y = over_x(send_x), over_y(send_y)
    from_x, from_y, from_xy, peer_output, out_x = after((from_x, from_y, from_xy, peer_output, out_x))
    own, send, send_q = call(
        backward_kernel,
        (
            shape((3 * rows, part), BF16),
            shape((5 * rows // 2, part), BF16),
            shape((rows // 2, part), BF16),
        ),
        (counts, q, k, v, probs, output, keep, from_x, from_y, from_xy),
        smem=(0,),
        scratch=(pltpu.VMEM((total, part), BF16), pltpu.VMEM((3, total, part), BF16)),
    )
    peer = over_y(send)
    near_g, peer_second, peer_output, peer_first_z = after(
        (near_g, peer_second, peer_output, peer_first_z, send)
    )[:4]
    near_g = over_core(near_g)
    peer_second_z = over_z(peer_second)
    peer_x = over_x(peer_output)
    bundled = (
        peer_first, peer_first_z, peer_second, peer_second_z, output, out_x, peer_output, peer_x
    )
    *bundled, peer, send_q = after((*bundled, peer, send_q))
    peer_q = over_y(send_q)
    own_p, bundle = call(
        bundle_kernel,
        (shape((total, width), BF16), shape((3 * total, width), BF16)),
        bundled,
    )
    bundle = over_core(bundle)
    operands = (pltpu.VMEM((2 * total, width), BF16), pltpu.VMEM((2 * total, width), BF16))
    weight_grad = call(
        own_weight_kernel,
        shape(out_weight.shape, BF16),
        (own_g, own_p, output, out_x, peer_output, peer_x),
        scratch=operands,
    )
    weight_grad = call(
        weight_kernel,
        shape(out_weight.shape, F32),
        (weight_grad, near_g, bundle),
        out=pl.ANY,
        scratch=(
            *operands,
            pltpu.VMEM((4, width // 4, width), F32),
            pltpu.SemaphoreType.DMA((4,)),
        ),
        vmem=8,
    )
    weight_grad, own = after((weight_grad, own))
    grads = call(
        finish_kernel,
        tuple(shape((rows, width), BF16) for _ in range(3)),
        (own, peer, peer_q),
        out=pl.ANY,
        scratch=(pltpu.SemaphoreType.DMA((3, 3)),),
    )
    return (grads[0][None], grads[1][None], grads[2][None], weight_grad)


def general_device(queries, keys, values, out_grad, out_weight, slopes, counts, gaps):
    row_count = queries.shape[1]
    width = queries.shape[2]
    head_count = slopes.shape[0]
    head_size = width // head_count
    scaling = head_size ** (-0.5)
    shard_count = lax.axis_size("context")
    my_start = lax.axis_index("context") * row_count
    total_slots = shard_count * row_count
    all_gaps, all_counts = (
        lax.all_gather(gaps, "context", axis=1, tiled=True),
        lax.all_gather(counts, "context", axis=1, tiled=True),
    )
    slot_index = jnp.arange(total_slots, dtype=jnp.int32)
    owner = slot_index // row_count
    shard_ids = jnp.arange(shard_count, dtype=jnp.int32)
    slot_limit = jnp.sum(
        jnp.where(owner[:, None] == shard_ids[None, :], all_counts[0][None, :], 0), axis=1
    )
    slot_valid = slot_index % row_count < slot_limit
    offsets = jnp.cumsum(jnp.where(slot_valid, all_gaps[0], 0)).astype(jnp.float32)
    my_valid = lax.dynamic_slice_in_dim(slot_valid, my_start, row_count)
    grad_full = lax.all_gather(out_grad[0], "tensor", axis=1, tiled=True)
    grad_masked = jnp.where(my_valid[:, None], grad_full, jnp.zeros_like(grad_full))
    columns = grad_masked
    grad_heads = jnp.dot(
        columns,
        lax.all_gather(out_weight, "fsdp", axis=0, tiled=True),
        preferred_element_type=jnp.float32,
    ).astype(jnp.bfloat16)
    local_q = queries[0]
    local_k = keys[0]
    local_v = values[0]
    key_full, value_full = (
        lax.all_gather(local_k, "context", axis=0, tiled=True),
        lax.all_gather(local_v, "context", axis=0, tiled=True),
    )

    def split(block):
        return block.reshape(block.shape[0], head_count, head_size)

    def scores(q_block, q_start, k_block, k_start):
        query_count = q_block.shape[0]
        key_count = k_block.shape[0]
        logits = (
            jnp.einsum(
                "qhd,khd->hqk", split(q_block), split(k_block), preferred_element_type=jnp.float32
            )
            * scaling
        )
        q_offset = lax.dynamic_slice_in_dim(offsets, q_start, query_count)
        k_offset = lax.dynamic_slice_in_dim(offsets, k_start, key_count)
        k_valid = lax.dynamic_slice_in_dim(slot_valid, k_start, key_count)
        q_slot = q_start + jnp.arange(query_count, dtype=jnp.int32)
        k_slot = k_start + jnp.arange(key_count, dtype=jnp.int32)
        allowed = k_valid[None, :] & (k_slot[None, :] <= q_slot[:, None])
        logits = logits - slopes[:, None, None] * (
            q_offset[None, :, None] - k_offset[None, None, :]
        )
        return (jnp.where(allowed[None], logits, NEG), allowed)

    def tile_terms(q_block, g_block, q_lse, q_delta, q_start, k_block, v_block, k_start):
        logits, allowed = scores(q_block, q_start, k_block, k_start)
        probs = jnp.where(allowed[None], jnp.exp(logits - q_lse[:, :, None]), 0.0)
        value_dots = jnp.einsum(
            "qhd,khd->hqk", split(g_block), split(v_block), preferred_element_type=jnp.float32
        )
        dscore = (probs * (value_dots - q_delta[:, :, None])).astype(jnp.bfloat16)
        return (probs.astype(jnp.bfloat16), dscore)

    block = 2 * row_count
    block_total = total_slots // block

    def mass_step(block_index, carry):
        k_start = block_index * block
        k_block = lax.dynamic_slice_in_dim(key_full, k_start, block, 0)

        def work(state):
            peak, mass = state
            logits, allowed = scores(local_q, my_start, k_block, k_start)
            new_peak = jnp.maximum(peak, jnp.max(logits, axis=2))
            weights = jnp.where(allowed[None], jnp.exp(logits - new_peak[:, :, None]), 0.0)
            return (new_peak, mass * jnp.exp(peak - new_peak) + jnp.sum(weights, axis=2))

        return work(carry)

    start_state = (
        jnp.full((head_count, row_count), NEG, jnp.float32),
        jnp.zeros((head_count, row_count), jnp.float32),
    )
    peak, mass = lax.fori_loop(0, block_total, mass_step, start_state)
    log_total = peak + jnp.log(mass)

    def output_step(block_index, carry):
        k_start = block_index * block
        k_block = lax.dynamic_slice_in_dim(key_full, k_start, block, 0)
        v_block = lax.dynamic_slice_in_dim(value_full, k_start, block, 0)

        def work(acc):
            logits, allowed = scores(local_q, my_start, k_block, k_start)
            probs_b = jnp.where(allowed[None], jnp.exp(logits - log_total[:, :, None]), 0.0).astype(
                jnp.bfloat16
            )
            return acc + jnp.einsum(
                "hqk,khd->qhd", probs_b, split(v_block), preferred_element_type=jnp.float32
            ).reshape(row_count, width)

        return work(carry)

    output_b = lax.fori_loop(
        0, block_total, output_step, jnp.zeros((row_count, width), jnp.float32)
    ).astype(jnp.bfloat16)
    delta = jnp.sum(
        (grad_heads.astype(jnp.float32) * output_b.astype(jnp.float32)).reshape(
            row_count, head_count, head_size
        ),
        axis=2,
    ).T

    def query_step(block_index, carry):
        k_start = block_index * block
        k_block = lax.dynamic_slice_in_dim(key_full, k_start, block, 0)
        v_block = lax.dynamic_slice_in_dim(value_full, k_start, block, 0)

        def work(acc):
            probs_b, dscore = tile_terms(
                local_q, grad_heads, log_total, delta, my_start, k_block, v_block, k_start
            )
            return (
                acc
                + jnp.einsum(
                    "hqk,khd->qhd", dscore, split(k_block), preferred_element_type=jnp.float32
                ).reshape(row_count, width)
                * scaling
            )

        return work(carry)

    query_grad = lax.fori_loop(
        0, block_total, query_step, jnp.zeros((row_count, width), jnp.float32)
    ).astype(jnp.bfloat16)
    stats_lse, stats_delta = (
        lax.all_gather(log_total, "context", axis=1, tiled=True),
        lax.all_gather(delta, "context", axis=1, tiled=True),
    )
    start = jnp.int32(0)
    q_piece = lax.all_gather(local_q, "context", axis=0, tiled=True)
    g_piece = lax.all_gather(grad_heads, "context", axis=0, tiled=True)

    def work(held):
        probs_b, dscore = tile_terms(
            q_piece, g_piece, stats_lse, stats_delta, start, local_k, local_v, my_start
        )
        key_part = (
            jnp.einsum(
                "hqk,qhd->khd", dscore, split(q_piece), preferred_element_type=jnp.float32
            ).reshape(row_count, width)
            * scaling
        )
        value_part = jnp.einsum(
            "hqk,qhd->khd", probs_b, split(g_piece), preferred_element_type=jnp.float32
        ).reshape(row_count, width)
        return jnp.concatenate([key_part, value_part], axis=1)

    key_value_grads = work(jnp.zeros((row_count, 2 * width), jnp.float32))
    key_grad = key_value_grads[:, :width].astype(jnp.bfloat16)
    value_grad = key_value_grads[:, width:].astype(jnp.bfloat16)
    columns = grad_masked
    weight_share = lax.psum_scatter(
        lax.dot_general(
            columns, output_b, (((0,), (0,)), ((), ())), preferred_element_type=jnp.float32
        ),
        "fsdp",
        scatter_dimension=0,
        tiled=True,
    )
    weight_grad = lax.psum(weight_share, "context")
    return (query_grad[None], key_grad[None], value_grad[None], weight_grad)


def solution(mesh):
    placed = (
        P("fsdp", "context", "tensor"),
        P("fsdp", "context", "tensor"),
        P("fsdp", "context", "tensor"),
        P("fsdp", "context", "tensor"),
        P("fsdp", "tensor"),
        P("tensor"),
        P("fsdp", "context"),
        P("fsdp", "context"),
    )
    sizes = dict(mesh.shape)
    packs = sizes["context"] == 2 and sizes["tensor"] == 4 and sizes["fsdp"] == 4
    return jax.shard_map(
        packed_device if packs else general_device,
        mesh=mesh,
        in_specs=placed,
        out_specs=(
            P("fsdp", "context", "tensor"),
            P("fsdp", "context", "tensor"),
            P("fsdp", "context", "tensor"),
            P("fsdp", "tensor"),
        ),
        check_vma=False,
    )
```

```python
import functools

import jax
import jax.numpy as jnp
from jax import lax
from jax.experimental import pallas as pl
from jax.experimental.pallas import tpu as pltpu
from jax.sharding import PartitionSpec as P

NEG = -1e30
F32 = jnp.float32
BF16 = jnp.bfloat16
NN = (((1,), (0,)), ((), ()))
NT = (((1,), (1,)), ((), ()))
TN = (((0,), (0,)), ((), ()))


def dot(a, b, dims=NN):
    return lax.dot_general(a, b, dims, preferred_element_type=F32)


def iota(shape, axis):
    return lax.broadcasted_iota(jnp.int32, shape, axis)


def onehot(mask):
    return jnp.where(mask, 1.0, 0.0).astype(BF16)


def call(body, outs, args, smem=(), out=pltpu.VMEM, scratch=(), vmem=8):
    return pl.pallas_call(
        body,
        out_shape=outs,
        in_specs=[
            pl.BlockSpec(memory_space=pltpu.SMEM if i in smem else pltpu.VMEM)
            for i in range(len(args))
        ],
        out_specs=jax.tree.map(lambda _: pl.BlockSpec(memory_space=out), outs),
        scratch_shapes=list(scratch),
        compiler_params=pltpu.CompilerParams(vmem_limit_bytes=vmem * 2**20),
    )(*args)


def packed_slot(index, half, rows, count0, count1):
    own0 = jnp.where(index < count0, index, rows + half + index - count0)
    other = index - half
    own1 = jnp.where(other < count1, rows + other, half + other - count1)
    return jnp.where(index < half, own0, own1)


def pack_rows_kernel(count_ref, own_ref, extra_ref, out_ref):
    half = out_ref.shape[0]
    extra = extra_ref.shape[0]
    count = count_ref[0, 0]
    at, row = iota((half, half), 0), iota((half, half), 1)
    first = onehot((at == row) & (at < count))
    at, row = iota((half, extra), 0), iota((half, extra), 1)
    second = onehot((at >= count) & (at - count == row))
    out_ref[...] = (dot(first, own_ref[...]) + dot(second, extra_ref[...])).astype(BF16)


def forward_kernel(
    count_ref, slopes_ref, mine_ref, message_ref, q_out, k_out, v_out, probs_out, output_ref
):
    part = mine_ref.shape[1]
    rows = (mine_ref.shape[0] - 16) // 3
    total = q_out.shape[0]
    half = total // 2
    heads = probs_out.shape[0]
    size = part // heads
    c = lax.axis_index("context")
    count = count_ref[0, 0]
    count0 = jnp.where(c == 0, count, total - count)
    count1 = total - count0
    slot_down = packed_slot(iota((total, rows), 0), half, rows, count0, count1)
    slot_here = iota((total, rows), 1)
    own_slot = c * rows + slot_here
    peer_slot = (1 - c) * rows + slot_here
    own_pick, peer_pick = onehot(slot_down == own_slot), onehot(slot_down == peer_slot)
    own_until = onehot((own_slot <= slot_down) & (slot_here < count))
    peer_until = onehot((peer_slot <= slot_down) & (slot_here < total - count))
    own_gaps = mine_ref[3 * rows :, :rows]
    peer_gaps = message_ref[3 * rows :, :rows]
    offset_down = (dot(own_until, own_gaps, NT) + dot(peer_until, peer_gaps, NT))[:, :1]
    offset_across = (dot(own_gaps, own_until, NT) + dot(peer_gaps, peer_until, NT))[:1, :]
    slot_q = packed_slot(iota((total, total), 0), half, rows, count0, count1)
    slot_k = packed_slot(iota((total, total), 1), half, rows, count0, count1)
    allowed = slot_k <= slot_q
    distance = offset_down - offset_across
    for n, out in enumerate((q_out, k_out, v_out)):
        at = slice(n * rows, (n + 1) * rows)
        out[...] = (dot(own_pick, mine_ref[at, :]) + dot(peer_pick, message_ref[at, :])).astype(BF16)
    for h in range(heads):
        cols = slice(h * size, (h + 1) * size)
        slope = slopes_ref[c * heads + h]
        score = dot(q_out[:, cols], k_out[:, cols], NT) * (size**-0.5) - slope * distance
        score = jnp.where(allowed, score, NEG)
        peak = jnp.max(score, axis=1, keepdims=True)
        mass = jnp.where(allowed, jnp.exp(score - peak), 0.0)
        probs = mass / jnp.sum(mass, axis=1, keepdims=True)
        probs_out[h] = probs
        output_ref[:, cols] = dot(probs.astype(BF16), v_out[:, cols]).astype(BF16)


def place(blocks, own_ref, near_ref):
    half = own_ref.shape[0] // 2
    t, f = lax.axis_index("tensor"), lax.axis_index("fsdp")
    h, l, x, core = t // 2, t % 2, f // 2, f % 2
    swap_seq = (h + x) % 2
    swap_chunk = (l + core) % 2
    for seq in range(2):
        for chunk in range(2):

            @pl.when((swap_seq == seq) & (swap_chunk == chunk))
            def _(seq=seq, chunk=chunk):
                for n in range(2):
                    at = slice(n * half, (n + 1) * half)
                    own_ref[at, :] = blocks[n ^ seq][chunk][...]
                    near_ref[at, :] = blocks[n ^ seq][1 - chunk][...]


def bundle_kernel(
    p00_ref, p01_ref, p10_ref, p11_ref, mine_ref, mine_x_ref, away_ref, away_x_ref,
    own_p_ref, bundle_ref,
):
    pair, part = mine_ref.shape
    blocks = (p00_ref, p01_ref), (p10_ref, p11_ref)
    place(blocks, own_p_ref, bundle_ref.at[:pair])
    bundle_ref[pair : 2 * pair, :part] = mine_ref[...]
    bundle_ref[pair : 2 * pair, part:] = mine_x_ref[...]
    bundle_ref[2 * pair :, :part] = away_ref[...]
    bundle_ref[2 * pair :, part:] = away_x_ref[...]


def partial_kernel(
    b00_ref, b01_ref, b10_ref, b11_ref, own_w_ref, near_w_ref,
    keep_ref, send_x_ref, send_y_ref, send_xy_ref, own_g_ref, near_g_ref, total_ref,
):
    half, part = keep_ref.shape
    place(((b00_ref, b01_ref), (b10_ref, b11_ref)), own_g_ref, near_g_ref)
    total_ref[...] = dot(own_g_ref[...], own_w_ref[...]) + dot(near_g_ref[...], near_w_ref[...])
    c = lax.axis_index("context")
    mine = pl.ds(pl.multiple_of(c * part, part), part)
    away = pl.ds(pl.multiple_of((1 - c) * part, part), part)
    keep_ref[...] = total_ref[:half, mine]
    send_x_ref[...] = total_ref[half:, mine].astype(BF16)
    send_y_ref[...] = total_ref[:half, away].astype(BF16)
    send_xy_ref[...] = total_ref[half:, away].astype(BF16)


def backward_kernel(
    count_ref, q_ref, k_ref, v_ref, probs_ref, output_ref, keep_ref, from_x_ref, from_y_ref, from_xy_ref,
    own_ref, send_ref, send_q_ref, g_ref, grads_ref,
):
    total, part = q_ref.shape
    half = total // 2
    heads = probs_ref.shape[0]
    size = part // heads
    rows = own_ref.shape[0] // 3
    c = lax.axis_index("context")
    count = count_ref[0, 0]
    count0 = jnp.where(c == 0, count, total - count)
    here = (keep_ref[...] + from_x_ref[...].astype(F32)).astype(BF16)
    there = (from_y_ref[...].astype(F32) + from_xy_ref[...].astype(F32)).astype(BF16)
    g_ref[pl.ds(pl.multiple_of(c * half, half), half), :] = here
    g_ref[pl.ds(pl.multiple_of((1 - c) * half, half), half), :] = there
    for h in range(heads):
        cols = slice(h * size, (h + 1) * size)
        probs = probs_ref[h]
        g, q, k, v = g_ref[:, cols], q_ref[:, cols], k_ref[:, cols], v_ref[:, cols]
        delta = jnp.sum(g.astype(F32) * output_ref[:, cols].astype(F32), axis=1, keepdims=True)
        dscore = (probs * (dot(g, v, NT) - delta)).astype(BF16)
        grads_ref[0, :, cols] = (dot(dscore, k) * (size**-0.5)).astype(BF16)
        grads_ref[1, :, cols] = (dot(dscore, q, TN) * (size**-0.5)).astype(BF16)
        grads_ref[2, :, cols] = dot(probs.astype(BF16), g, TN).astype(BF16)
    slot = packed_slot(iota((rows, total), 1), half, rows, count0, total - count0)
    row = iota((rows, total), 0)
    own_pick, peer_pick = onehot(slot == c * rows + row), onehot(slot == (1 - c) * rows + row)
    cut = send_q_ref.shape[0]
    picked = dot(peer_pick, grads_ref[0]).astype(BF16)
    send_q_ref[...] = picked[:cut]
    send_ref[2 * rows :, :] = picked[cut:]
    for n in range(1, 3):
        send_ref[(n - 1) * rows : n * rows, :] = dot(peer_pick, grads_ref[n]).astype(BF16)
    for n in range(3):
        own_ref[n * rows : (n + 1) * rows, :] = dot(own_pick, grads_ref[n]).astype(BF16)


def finish_kernel(own_ref, peer_ref, peer_q_ref, q_ref, k_ref, v_ref, sems):
    rows, width = q_ref.shape
    part = width // 2
    c = lax.axis_index("context")
    copies = []
    own = [own_ref.at[n * rows : (n + 1) * rows, :] for n in range(3)]
    cut = peer_q_ref.shape[0]
    peer = [peer_q_ref, peer_ref.at[:rows, :], peer_ref.at[rows : 2 * rows, :]]
    for side, sources in enumerate((own, peer)):
        at = pl.ds(pl.multiple_of((c if side == 0 else 1 - c) * part, part), part)
        for n, ref in enumerate((q_ref, k_ref, v_ref)):
            to = ref.at[:cut, at] if side == 1 and n == 0 else ref.at[:, at]
            copies.append(pltpu.make_async_copy(sources[n], to, sems.at[side, n]))
    rest = q_ref.at[cut:, pl.ds(pl.multiple_of((1 - c) * part, part), part)]
    copies.append(pltpu.make_async_copy(peer_ref.at[2 * rows :, :], rest, sems.at[2, 0]))
    for copy in copies:
        copy.start()
    for copy in copies:
        copy.wait()


def weight_operands(grads, outputs, left_ref, right_ref):
    pair = grads[0].shape[0]
    half, part = pair // 2, right_ref.shape[1] // 2
    c = lax.axis_index("context")
    for which, ref in enumerate(grads):
        for s in range(2):
            row = s * pair + (c if which == 0 else 1 - c) * half
            left_ref[pl.ds(pl.multiple_of(row, half), half), :] = ref[s * half : (s + 1) * half, :]
    for side, refs in enumerate(outputs):
        at = pl.ds(pl.multiple_of((c if side == 0 else 1 - c) * part, part), part)
        for s, ref in enumerate(refs):
            right_ref[s * pair : (s + 1) * pair, at] = ref[...]


def own_weight_kernel(
    own_g_ref, own_p_ref, mine_ref, mine_x_ref, away_ref, away_x_ref,
    total_ref, left_ref, right_ref,
):
    outputs = (mine_ref, mine_x_ref), (away_ref, away_x_ref)
    weight_operands((own_g_ref, own_p_ref), outputs, left_ref, right_ref)
    block = left_ref.shape[1] // 4
    for n in range(4):
        rows = slice(n * block, (n + 1) * block)
        total_ref[rows, :] = dot(left_ref[:, rows], right_ref[...], TN).astype(BF16)


def weight_kernel(
    total_ref, near_g_ref, bundle_ref, weight_ref, left_ref, right_ref, done_ref, sems
):
    pair, part = near_g_ref.shape[0], near_g_ref.shape[1] // 2
    outputs = [
        [bundle_ref.at[n * pair : (n + 1) * pair, s * part : (s + 1) * part] for s in range(2)]
        for n in (1, 2)
    ]
    weight_operands((near_g_ref, bundle_ref.at[:pair]), outputs, left_ref, right_ref)
    blocks, block = done_ref.shape[:2]
    copies = []
    for n in range(blocks):
        rows = slice(n * block, (n + 1) * block)
        done_ref[n] = total_ref[rows, :].astype(F32) + dot(left_ref[:, rows], right_ref[...], TN)
        copies.append(pltpu.make_async_copy(done_ref.at[n], weight_ref.at[rows, :], sems.at[n]))
        copies[-1].start()
    for copy in copies:
        copy.wait()


def spread(flip):
    pairs = []
    for t in range(4):
        for f in range(4):
            h, l, x, core = t >> 1, t & 1, f >> 1, f & 1
            pairs.append((t * 4 + f, ((x ^ flip) << 1 | l) * 4 + (h << 1 | core)))
    return pairs


def packed_device(queries, keys, values, out_grad, out_weight, slopes, counts, gaps):
    rows, width = queries.shape[1:]
    part = width // 2
    total = 2 * rows * 5 // 8
    half = total // 2
    heads = slopes.shape[0] // 2
    shape = jax.ShapeDtypeStruct
    over_y = lambda a: lax.ppermute(a, "context", [(0, 1), (1, 0)])
    over_x = lambda a: lax.ppermute(a, "fsdp", [(i, i ^ 2) for i in range(4)])
    over_core = lambda a: lax.ppermute(a, "fsdp", [(i, i ^ 1) for i in range(4)])
    after = lax.optimization_barrier

    grad = out_grad[0]
    c = lax.axis_index("context")

    def side(which, q, k, v):
        cut = lambda a: lax.dynamic_slice_in_dim(a[0], which * part, part, 1)
        return jnp.concatenate([cut(q), cut(k), cut(v), tail], axis=0)

    extra, gaps, near_weight, *source = after(
        (grad[half:], gaps, out_weight, queries, keys, values)
    )
    near_weight = over_core(near_weight)
    extra = over_y(extra)
    tail = jnp.broadcast_to(gaps.astype(BF16), (16, rows))
    tail = jnp.concatenate([tail] * (part // rows), axis=1)
    message = side(1 - c, *source)
    packed = call(
        pack_rows_kernel, shape((half, width), BF16), (counts, grad[:half], extra), smem=(0,)
    )
    message = over_y(message)
    packed, near_weight, *source = after((packed, near_weight, *source))
    mine = side(c, *source)
    first, second = [lax.ppermute(packed, ("tensor", "fsdp"), spread(a)) for a in (0, 1)]
    over_z = lambda a: lax.ppermute(a, "tensor", [(i, i ^ 1) for i in range(4)])
    blocks = [first, over_z(first), second, over_z(second)]
    q, k, v, probs, output = call(
        forward_kernel,
        (
            shape((total, part), BF16),
            shape((total, part), BF16),
            shape((total, part), BF16),
            shape((heads, total, total), F32),
            shape((total, part), BF16),
        ),
        (counts, slopes, mine, message),
        smem=(0, 1),
    )
    out_x = over_x(output)
    peer_output = over_y(output)
    peer_first, peer_second = over_y(first), over_y(second)
    peer_second_z = over_z(peer_second)
    *blocks, output, peer_second = after((*blocks, output, peer_second))
    keep, send_x, send_y, send_xy, own_g, near_g = call(
        partial_kernel,
        (
            shape((half, part), F32),
            shape((half, part), BF16),
            shape((half, part), BF16),
            shape((half, part), BF16),
            shape((total, width), BF16),
            shape((total, width), BF16),
        ),
        (*blocks, out_weight, near_weight),
        scratch=(pltpu.VMEM((total, width), F32),),
    )
    from_xy = lax.ppermute(
        send_xy,
        ("context", "fsdp"),
        [(c * 4 + f, (1 - c) * 4 + (f ^ 2)) for c in range(2) for f in range(4)],
    )
    from_x, from_y = over_x(send_x), over_y(send_y)
    from_x, from_y, from_xy, peer_output, out_x, peer_first = after(
        (from_x, from_y, from_xy, peer_output, out_x, peer_first)
    )
    own, send, send_q = call(
        backward_kernel,
        (
            shape((3 * rows, part), BF16),
            shape((5 * rows // 2, part), BF16),
            shape((rows // 2, part), BF16),
        ),
        (counts, q, k, v, probs, output, keep, from_x, from_y, from_xy),
        smem=(0,),
        scratch=(pltpu.VMEM((total, part), BF16), pltpu.VMEM((3, total, part), BF16)),
    )
    peer = over_y(send)
    near_g, peer_first, peer_output, peer_second_z = after(
        (near_g, peer_first, peer_output, peer_second_z, send)
    )[:4]
    near_g = over_core(near_g)
    peer_first_z = over_z(peer_first)
    peer_x = over_x(peer_output)
    bundled = (
        peer_first, peer_first_z, peer_second, peer_second_z, output, out_x, peer_output, peer_x
    )
    *bundled, peer, send_q = after((*bundled, peer, send_q))
    peer_q = over_y(send_q)
    own_p, bundle = call(
        bundle_kernel,
        (shape((total, width), BF16), shape((3 * total, width), BF16)),
        bundled,
    )
    bundle = over_core(bundle)
    operands = (pltpu.VMEM((2 * total, width), BF16), pltpu.VMEM((2 * total, width), BF16))
    weight_grad = call(
        own_weight_kernel,
        shape(out_weight.shape, BF16),
        (own_g, own_p, output, out_x, peer_output, peer_x),
        scratch=operands,
    )
    weight_grad = call(
        weight_kernel,
        shape(out_weight.shape, F32),
        (weight_grad, near_g, bundle),
        out=pl.ANY,
        scratch=(
            *operands,
            pltpu.VMEM((8, width // 8, width), F32),
            pltpu.SemaphoreType.DMA((8,)),
        ),
        vmem=8,
    )
    weight_grad, own = after((weight_grad, own))
    grads = call(
        finish_kernel,
        tuple(shape((rows, width), BF16) for _ in range(3)),
        (own, peer, peer_q),
        out=pl.ANY,
        scratch=(pltpu.SemaphoreType.DMA((3, 3)),),
    )
    return (grads[0][None], grads[1][None], grads[2][None], weight_grad)


def general_device(queries, keys, values, out_grad, out_weight, slopes, counts, gaps):
    row_count = queries.shape[1]
    width = queries.shape[2]
    head_count = slopes.shape[0]
    head_size = width // head_count
    scaling = head_size ** (-0.5)
    shard_count = lax.axis_size("context")
    my_start = lax.axis_index("context") * row_count
    total_slots = shard_count * row_count
    all_gaps, all_counts = (
        lax.all_gather(gaps, "context", axis=1, tiled=True),
        lax.all_gather(counts, "context", axis=1, tiled=True),
    )
    slot_index = jnp.arange(total_slots, dtype=jnp.int32)
    owner = slot_index // row_count
    shard_ids = jnp.arange(shard_count, dtype=jnp.int32)
    slot_limit = jnp.sum(
        jnp.where(owner[:, None] == shard_ids[None, :], all_counts[0][None, :], 0), axis=1
    )
    slot_valid = slot_index % row_count < slot_limit
    offsets = jnp.cumsum(jnp.where(slot_valid, all_gaps[0], 0)).astype(jnp.float32)
    my_valid = lax.dynamic_slice_in_dim(slot_valid, my_start, row_count)
    grad_full = lax.all_gather(out_grad[0], "tensor", axis=1, tiled=True)
    grad_masked = jnp.where(my_valid[:, None], grad_full, jnp.zeros_like(grad_full))
    columns = grad_masked
    grad_heads = jnp.dot(
        columns,
        lax.all_gather(out_weight, "fsdp", axis=0, tiled=True),
        preferred_element_type=jnp.float32,
    ).astype(jnp.bfloat16)
    local_q = queries[0]
    local_k = keys[0]
    local_v = values[0]
    key_full, value_full = (
        lax.all_gather(local_k, "context", axis=0, tiled=True),
        lax.all_gather(local_v, "context", axis=0, tiled=True),
    )

    def split(block):
        return block.reshape(block.shape[0], head_count, head_size)

    def scores(q_block, q_start, k_block, k_start):
        query_count = q_block.shape[0]
        key_count = k_block.shape[0]
        logits = (
            jnp.einsum(
                "qhd,khd->hqk", split(q_block), split(k_block), preferred_element_type=jnp.float32
            )
            * scaling
        )
        q_offset = lax.dynamic_slice_in_dim(offsets, q_start, query_count)
        k_offset = lax.dynamic_slice_in_dim(offsets, k_start, key_count)
        k_valid = lax.dynamic_slice_in_dim(slot_valid, k_start, key_count)
        q_slot = q_start + jnp.arange(query_count, dtype=jnp.int32)
        k_slot = k_start + jnp.arange(key_count, dtype=jnp.int32)
        allowed = k_valid[None, :] & (k_slot[None, :] <= q_slot[:, None])
        logits = logits - slopes[:, None, None] * (
            q_offset[None, :, None] - k_offset[None, None, :]
        )
        return (jnp.where(allowed[None], logits, NEG), allowed)

    def tile_terms(q_block, g_block, q_lse, q_delta, q_start, k_block, v_block, k_start):
        logits, allowed = scores(q_block, q_start, k_block, k_start)
        probs = jnp.where(allowed[None], jnp.exp(logits - q_lse[:, :, None]), 0.0)
        value_dots = jnp.einsum(
            "qhd,khd->hqk", split(g_block), split(v_block), preferred_element_type=jnp.float32
        )
        dscore = (probs * (value_dots - q_delta[:, :, None])).astype(jnp.bfloat16)
        return (probs.astype(jnp.bfloat16), dscore)

    block = 2 * row_count
    block_total = total_slots // block

    def mass_step(block_index, carry):
        k_start = block_index * block
        k_block = lax.dynamic_slice_in_dim(key_full, k_start, block, 0)

        def work(state):
            peak, mass = state
            logits, allowed = scores(local_q, my_start, k_block, k_start)
            new_peak = jnp.maximum(peak, jnp.max(logits, axis=2))
            weights = jnp.where(allowed[None], jnp.exp(logits - new_peak[:, :, None]), 0.0)
            return (new_peak, mass * jnp.exp(peak - new_peak) + jnp.sum(weights, axis=2))

        return work(carry)

    start_state = (
        jnp.full((head_count, row_count), NEG, jnp.float32),
        jnp.zeros((head_count, row_count), jnp.float32),
    )
    peak, mass = lax.fori_loop(0, block_total, mass_step, start_state)
    log_total = peak + jnp.log(mass)

    def output_step(block_index, carry):
        k_start = block_index * block
        k_block = lax.dynamic_slice_in_dim(key_full, k_start, block, 0)
        v_block = lax.dynamic_slice_in_dim(value_full, k_start, block, 0)

        def work(acc):
            logits, allowed = scores(local_q, my_start, k_block, k_start)
            probs_b = jnp.where(allowed[None], jnp.exp(logits - log_total[:, :, None]), 0.0).astype(
                jnp.bfloat16
            )
            return acc + jnp.einsum(
                "hqk,khd->qhd", probs_b, split(v_block), preferred_element_type=jnp.float32
            ).reshape(row_count, width)

        return work(carry)

    output_b = lax.fori_loop(
        0, block_total, output_step, jnp.zeros((row_count, width), jnp.float32)
    ).astype(jnp.bfloat16)
    delta = jnp.sum(
        (grad_heads.astype(jnp.float32) * output_b.astype(jnp.float32)).reshape(
            row_count, head_count, head_size
        ),
        axis=2,
    ).T

    def query_step(block_index, carry):
        k_start = block_index * block
        k_block = lax.dynamic_slice_in_dim(key_full, k_start, block, 0)
        v_block = lax.dynamic_slice_in_dim(value_full, k_start, block, 0)

        def work(acc):
            probs_b, dscore = tile_terms(
                local_q, grad_heads, log_total, delta, my_start, k_block, v_block, k_start
            )
            return (
                acc
                + jnp.einsum(
                    "hqk,khd->qhd", dscore, split(k_block), preferred_element_type=jnp.float32
                ).reshape(row_count, width)
                * scaling
            )

        return work(carry)

    query_grad = lax.fori_loop(
        0, block_total, query_step, jnp.zeros((row_count, width), jnp.float32)
    ).astype(jnp.bfloat16)
    stats_lse, stats_delta = (
        lax.all_gather(log_total, "context", axis=1, tiled=True),
        lax.all_gather(delta, "context", axis=1, tiled=True),
    )
    start = jnp.int32(0)
    q_piece = lax.all_gather(local_q, "context", axis=0, tiled=True)
    g_piece = lax.all_gather(grad_heads, "context", axis=0, tiled=True)

    def work(held):
        probs_b, dscore = tile_terms(
            q_piece, g_piece, stats_lse, stats_delta, start, local_k, local_v, my_start
        )
        key_part = (
            jnp.einsum(
                "hqk,qhd->khd", dscore, split(q_piece), preferred_element_type=jnp.float32
            ).reshape(row_count, width)
            * scaling
        )
        value_part = jnp.einsum(
            "hqk,qhd->khd", probs_b, split(g_piece), preferred_element_type=jnp.float32
        ).reshape(row_count, width)
        return jnp.concatenate([key_part, value_part], axis=1)

    key_value_grads = work(jnp.zeros((row_count, 2 * width), jnp.float32))
    key_grad = key_value_grads[:, :width].astype(jnp.bfloat16)
    value_grad = key_value_grads[:, width:].astype(jnp.bfloat16)
    columns = grad_masked
    weight_share = lax.psum_scatter(
        lax.dot_general(
            columns, output_b, (((0,), (0,)), ((), ())), preferred_element_type=jnp.float32
        ),
        "fsdp",
        scatter_dimension=0,
        tiled=True,
    )
    weight_grad = lax.psum(weight_share, "context")
    return (query_grad[None], key_grad[None], value_grad[None], weight_grad)


def solution(mesh):
    placed = (
        P("fsdp", "context", "tensor"),
        P("fsdp", "context", "tensor"),
        P("fsdp", "context", "tensor"),
        P("fsdp", "context", "tensor"),
        P("fsdp", "tensor"),
        P("tensor"),
        P("fsdp", "context"),
        P("fsdp", "context"),
    )
    sizes = dict(mesh.shape)
    packs = sizes["context"] == 2 and sizes["tensor"] == 4 and sizes["fsdp"] == 4
    return jax.shard_map(
        packed_device if packs else general_device,
        mesh=mesh,
        in_specs=placed,
        out_specs=(
            P("fsdp", "context", "tensor"),
            P("fsdp", "context", "tensor"),
            P("fsdp", "context", "tensor"),
            P("fsdp", "tensor"),
        ),
        check_vma=False,
    )
```
